128 devices in a mesh: dp: 4 (over x), fsdp: 32 (over y, z, core).
Axes of the slice: x: 4, y: 4, z: 4, core: 2. Of those that a mesh axis runs over, the one named last changes fastest.
Arguments:
- log_mel: bfloat16 [16384, 16, 128], P(('dp', 'fsdp')), may hold values from -10 to 10
- bucket_list: int32 [128, 128], P(('dp', 'fsdp')), may hold values from 0 to 127, each once within a row
- utterance_frames: int32 [512], P(('dp', 'fsdp')), may hold values from 256 to 512
- stem_weight: bfloat16 [16, 48], replicated, may hold values from -3 to 3
- first_gain: float32 [1536], replicated, may hold values from 0.5 to 1.5
- gate_proj: bfloat16 [1536, 3072], P('fsdp'), may hold values from -0.15625 to 0.15625
- conv_kernel: float32 [31, 1536], replicated, may hold values from -3 to 3
- second_gain: float32 [1536], replicated, may hold values from 0.5 to 1.5
- out_proj: bfloat16 [1536, 1536], P('fsdp'), may hold values from -0.15625 to 0.15625
- cotangent: bfloat16 [65536, 1536], P(('dp', 'fsdp')), may hold values from -0.125 to 0.125
Outputs:
- output: bfloat16 [65536, 1536], P(('dp', 'fsdp'))
- grad_gate: float32 [1536, 3072], P('fsdp')
- grad_out: float32 [1536, 1536], P('fsdp')
- grad_stem: float32 [16, 48], replicated
- grad_first: float32 [1536], replicated
- grad_conv: float32 [31, 1536], replicated
- grad_second: float32 [1536], replicated
The draws below stay inside these ranges and needn't reach their ends.
Inputs may be any that keep to these rules, and one draw needn't show every extreme that they name: `bucket_list`: each row names each number once.
All inputs are finite; a program needn't handle non-finite values.
Results may differ from the reference program's by a relative error of at most 0.024.
Values may be sent and summed in bfloat16 or wider, within the bound.
No kernel may reach another device: no remote copies, remote signals or barrier semaphores. Data moves between devices by JAX's collectives and lax.ppermute only.
A program may use at most 320 MiB of HBM per device.

```python
from functools import partial
import jax
import jax.numpy as jnp
from jax import lax

D = 1536
MEL = 128
CONV_K = 31
PATCH = 4
TOK_DEV = 512
UTT_TOK = 128
PEERS = 128
STEM_CH = 48
TILE_FR = 16
NTILES = 16384
TOKENS = 65536
UTTS = 512


def spread_scales(key, number, lowest, highest):
    exponent = jax.random.uniform(key, (number,), jnp.float32, jnp.log(lowest), jnp.log(highest))
    return jnp.exp(exponent)


def draw_log_mel(key, part):
    key = jax.random.fold_in(key, 11)
    first_key, second_key = jax.random.split(key, 2)
    values = jnp.clip(jax.random.normal(first_key, (NTILES, TILE_FR, MEL), jnp.float32), -3.0, 3.0)
    scales = spread_scales(second_key, NTILES * TILE_FR, 0.3, 3.0).reshape(NTILES, TILE_FR, 1)
    return (values * scales).astype(jnp.bfloat16)


def draw_stem_weight(key, part):
    key = jax.random.fold_in(key, 23)
    first_key, second_key = jax.random.split(key, 2)
    values = jnp.clip(jax.random.normal(first_key, (PATCH * PATCH, STEM_CH), jnp.float32), -3.0, 3.0)
    scales = spread_scales(second_key, STEM_CH, 0.3, 3.0).reshape(1, STEM_CH)
    return (values * scales * 0.25).astype(jnp.bfloat16)


def draw_conv_kernel(key, part):
    key = jax.random.fold_in(key, 37)
    first_key, second_key = jax.random.split(key, 2)
    values = jnp.clip(jax.random.normal(first_key, (CONV_K, D), jnp.float32), -3.0, 3.0)
    scales = spread_scales(second_key, D, 0.3, 3.0).reshape(1, D)
    return values * scales * CONV_K ** (-0.5)


def place_ends(values, own_key, least, high):
    place = [jax.random.randint(jax.random.fold_in(own_key, axis), (), 0, length) for axis, length in enumerate(values.shape)]
    main_axis = values.shape.index(max(values.shape))
    beside = place[:main_axis] + [(place[main_axis] + 1) % values.shape[main_axis]] + place[main_axis + 1:]
    return values.at[tuple(place)].set(least).at[tuple(beside)].set(high)


def level_of(own_key, extent, pieces, least, high):
    level, own = 1.0, jax.random.fold_in(own_key, 6)
    for position, blocks in pieces:
        heights = jnp.exp(jax.random.uniform(jax.random.fold_in(own, position), (blocks,), jnp.float32, least / len(pieces), high / len(pieces)))
        level = level * jnp.repeat(heights, extent[position] // blocks).reshape([-1 if axis == position else 1 for axis in range(len(extent))])
    return level


def bell_draw(own_key, extent, scale, most, pieces=(), dtype=jnp.bfloat16):
    level = level_of(own_key, extent, pieces, -0.22, 0.18) if pieces else 1.0
    result = jax.random.normal(own_key, extent, jnp.float32) * scale * level
    return jnp.minimum(jnp.maximum(result, -most), most).astype(dtype)


def setup_inputs(seed: int = 0) -> dict:
    streams_of = jax.random.split(jax.random.key(seed), 11)
    log_mel = draw_log_mel(jax.random.fold_in(streams_of[10], 71), 0)
    bucket_list = jax.vmap(lambda own: jax.random.permutation(own, PEERS))(jax.random.split(streams_of[1], PEERS)).reshape((PEERS, PEERS)).astype(jnp.int32)
    utterance_frames = place_ends(jax.random.randint(streams_of[2], (UTTS,), PATCH * UTT_TOK // 2, PATCH * UTT_TOK + 1), jax.random.fold_in(streams_of[2], 1), PATCH * UTT_TOK // 2, PATCH * UTT_TOK).astype(jnp.int32)
    stem_weight = draw_stem_weight(jax.random.fold_in(streams_of[10], 71), 0)
    first_gain = jnp.clip(jax.random.uniform(streams_of[4], (D,), jnp.float32, 0.5, 1.5), 0.5, 1.5)
    gate_proj = bell_draw(streams_of[5], (D, 2 * D), D ** -0.5, 0.15625, ((0, 32),))
    conv_kernel = draw_conv_kernel(jax.random.fold_in(streams_of[10], 71), 0)
    second_gain = jnp.clip(jax.random.uniform(streams_of[7], (D,), jnp.float32, 0.5, 1.5), 0.5, 1.5)
    out_proj = bell_draw(streams_of[8], (D, D), D ** -0.5, 0.15625, ((0, 32),))
    cotangent = bell_draw(streams_of[9], (TOKENS, D), (2.0 / TOKENS ** 0.5), 0.125, ((0, 128),))
    return {"log_mel": log_mel, "bucket_list": bucket_list, "utterance_frames": utterance_frames, "stem_weight": stem_weight, "first_gain": first_gain, "gate_proj": gate_proj, "conv_kernel": conv_kernel, "second_gain": second_gain, "out_proj": out_proj, "cotangent": cotangent}


EPSILON = 1e-05

def norm_rows(values, gain):
    centre = lax.optimization_barrier(jnp.mean(values, axis=-1, keepdims=True))
    centred = values - centre
    spread = lax.optimization_barrier(jnp.mean(centred * centred, axis=-1, keepdims=True))
    return centred * lax.rsqrt(spread + EPSILON) * gain

def depthwise(blocks, conv_kernel):
    tap_count = conv_kernel.shape[0]
    half_width = tap_count // 2
    length = blocks.shape[1]
    padded = jnp.pad(blocks, ((0, 0), (half_width, half_width), (0, 0)))
    summed = jnp.zeros(blocks.shape, jnp.float32)
    for offset in range(tap_count):
        summed = summed + padded[:, offset:offset + length, :] * conv_kernel[offset]
    return summed

def middle(valid_mask, activated, conv_kernel, second_gain):
    features = conv_kernel.shape[1]
    gated = activated[:, :features] * jax.nn.sigmoid(activated[:, features:]) * valid_mask
    blocks = gated.reshape(-1, UTT_TOK, features)
    filtered = depthwise(blocks, conv_kernel).reshape(gated.shape)
    return jax.nn.silu(norm_rows(filtered, second_gain))

def token_mask(utterance_frames):
    positions = lax.broadcasted_iota(jnp.int32, (utterance_frames.shape[0], UTT_TOK), 1)
    limits = (utterance_frames // PATCH)[:, None]
    return (positions < limits).astype(jnp.float32).reshape(-1, 1)

def stem_sum(frames, stem_weight):
    rows = frames.shape[0]
    groups = frames.shape[1] // (PATCH * PATCH)
    split_in = frames.reshape(rows, PATCH, groups, PATCH).astype(jnp.float32)
    kernel = stem_weight.reshape(PATCH, PATCH, -1).astype(jnp.float32)
    summed = jnp.einsum('tigj,ijc->tgc', split_in, kernel)
    return summed.reshape(rows, -1)

def stem_weight_grad(frames, pre_grad):
    rows = frames.shape[0]
    groups = frames.shape[1] // (PATCH * PATCH)
    split_in = frames.reshape(rows, PATCH, groups, PATCH).astype(jnp.float32)
    split_grad = pre_grad.reshape(rows, groups, -1).astype(jnp.float32)
    summed = jnp.einsum('tigj,tgc->ijc', split_in, split_grad)
    return summed.reshape(PATCH * PATCH, -1)

def layer(frames, valid_mask, stem_weight, first_gain, gate_proj, conv_kernel, second_gain, out_proj, cotangent):
    stem_total = stem_sum(frames, stem_weight)
    embedded = jax.nn.silu(stem_total).astype(jnp.bfloat16) * valid_mask.astype(jnp.bfloat16)
    embed_wide = embedded.astype(jnp.float32)
    normed = norm_rows(embed_wide, first_gain).astype(jnp.bfloat16)
    activated = jnp.dot(normed, gate_proj, preferred_element_type=jnp.float32)
    swish_wide = middle(valid_mask, activated, conv_kernel, second_gain)
    swished = swish_wide.astype(jnp.bfloat16)
    mixed = jnp.dot(swished, out_proj, preferred_element_type=jnp.float32)
    output = ((embed_wide + mixed) * valid_mask).astype(jnp.bfloat16)
    mix_grad = cotangent * valid_mask.astype(jnp.bfloat16)
    swish_grad = jnp.dot(mix_grad, out_proj.T, preferred_element_type=jnp.float32)
    unused, middle_back = jax.vjp(partial(middle, valid_mask), activated, conv_kernel, second_gain)
    act_wide, conv_part, second_part = middle_back(swish_grad)
    act_grad = act_wide.astype(jnp.bfloat16)
    gate_part = jnp.dot(normed.T, act_grad, preferred_element_type=jnp.float32)
    out_part = jnp.dot(swished.T, mix_grad, preferred_element_type=jnp.float32)
    normed_grad = jnp.dot(act_grad, gate_proj.T, preferred_element_type=jnp.float32)
    unused, norm_back = jax.vjp(norm_rows, embed_wide, first_gain)
    embed_grad, first_part = norm_back(normed_grad)
    embed_grad = (embed_grad + mix_grad.astype(jnp.float32)) * valid_mask
    unused, silu_back = jax.vjp(jax.nn.silu, stem_total)
    pre_grad = silu_back(embed_grad)[0].astype(jnp.bfloat16)
    stem_part = stem_weight_grad(frames, pre_grad)
    return (output, (gate_part, out_part, stem_part, first_part, conv_part, second_part))

def rounded(values):
    return lax.optimization_barrier(values.astype(jnp.bfloat16)).astype(jnp.float32)

def pick_tiles(source_tiles, slot_order):
    return jnp.take(source_tiles, slot_order, axis=0)

def reference(log_mel, bucket_list, utterance_frames, stem_weight, first_gain, gate_proj, conv_kernel, second_gain, out_proj, cotangent):
    device_count = bucket_list.shape[0]
    by_source = log_mel.reshape(device_count, device_count, TILE_FR, MEL)
    chosen = jax.vmap(pick_tiles)(by_source, bucket_list)
    owners = jnp.swapaxes(chosen, 0, 1).reshape(device_count, TOK_DEV, PATCH * MEL)
    masks = token_mask(utterance_frames).reshape(device_count, TOK_DEV, 1)
    cot_rows = cotangent.reshape(device_count, TOK_DEV, D)
    starting = (jnp.zeros((D, 2 * D), jnp.float32), jnp.zeros((D, D), jnp.float32), jnp.zeros((PATCH * PATCH, STEM_CH), jnp.float32), jnp.zeros((D,), jnp.float32), jnp.zeros((CONV_K, D), jnp.float32), jnp.zeros((D,), jnp.float32))

    def owner_step(running, inputs):
        frames, valid_mask, cot_block = inputs
        output, parts = layer(frames, valid_mask, stem_weight, first_gain, gate_proj, conv_kernel, second_gain, out_proj, cot_block)
        updated = (running[0] + rounded(parts[0]), running[1] + rounded(parts[1]), running[2] + parts[2], running[3] + parts[3], running[4] + parts[4], running[5] + parts[5])
        return (updated, output)
    totals, outputs = lax.scan(owner_step, starting, (owners, masks, cot_rows))
    return (outputs.reshape(-1, D), totals[0], totals[1], totals[2], totals[3], totals[4], totals[5])
```

```python
import functools

import jax
import jax.numpy as jnp
import numpy as np
from jax import lax
from jax.experimental import pallas as pl
from jax.experimental.pallas import tpu as pltpu
from jax.sharding import Mesh
from jax.sharding import PartitionSpec as P

PATCH = 4
UTT = 128
TOK = 512
NU = TOK // UTT
D = 1536
MEL = 128
CH = 48
TAPS = 31
HALF = TAPS // 2
EPS = 1e-05
ROWS = 48
CB = 256
NB = D // CB
ALL = ("x", "y", "z", "c")
F32 = jnp.float32
BF16 = jnp.bfloat16
MIB = 1024 * 1024
COST = 1

CYC = 144
BINS = CYC // 2 + 1
IM = 80
SPEC = 160


def hi_lo(values):
    high = values.astype(np.float32).astype(jnp.bfloat16)
    low = (values - high.astype(np.float64)).astype(np.float32).astype(jnp.bfloat16)
    return high, low


def side_by_side(values, three=False):
    high, low = hi_lo(values)
    parts = [high, low] + ([high] if three else [])
    return np.concatenate(parts, axis=1)


def transforms():
    angle = 2 * np.pi / CYC
    bins = np.arange(BINS)[:, None]
    places = np.arange(UTT)[None, :]
    offsets = np.arange(TAPS)[None, :] - HALF
    forward = np.zeros((SPEC, UTT))
    forward[:BINS] = np.cos(angle * bins * places)
    forward[IM : IM + BINS] = -np.sin(angle * bins * places)
    kernel = np.zeros((SPEC, 32))
    kernel[:BINS, :TAPS] = np.cos(angle * bins * offsets)
    kernel[IM : IM + BINS, :TAPS] = np.sin(angle * bins * offsets)
    weight = np.full((BINS, 1), 2.0 / CYC)
    weight[0] = weight[-1] = 1.0 / CYC
    back = np.zeros((UTT, SPEC))
    back[:, :BINS] = (weight * np.cos(angle * bins * places)).T
    back[:, IM : IM + BINS] = -(weight * np.sin(angle * bins * places)).T
    return {
        "fwd": side_by_side(forward),
        "inv": side_by_side(back),
        "fwd_t": side_by_side(forward.T),
        "inv_t": side_by_side(back.T),
        "ker": side_by_side(kernel, True),
        "ker_t": side_by_side(kernel.T, True),
    }


def twice(values):
    narrow = values.astype(BF16)
    return jnp.concatenate([narrow, narrow], axis=0)


def thrice(values):
    high = values.astype(BF16)
    low = (values - high.astype(F32)).astype(BF16)
    return jnp.concatenate([high, high, low], axis=0)


def mm(left, right):
    return jnp.dot(left, right, preferred_element_type=F32)


def mm_nt(left, right):
    return lax.dot_general(left, right, (((1,), (1,)), ((), ())), preferred_element_type=F32)


def keep(limit, shape):
    return lax.broadcasted_iota(jnp.int32, shape, 0) < limit


def row_mean(values):
    return jnp.sum(values, axis=-1, keepdims=True) * (1.0 / D)


def normalise(values):
    centred = values - row_mean(values)
    scale = lax.rsqrt(row_mean(centred * centred) + EPS)
    return centred * scale, scale


def normalise_back(grad, unit, scale):
    return scale * (grad - row_mean(grad) - unit * row_mean(grad * unit))


def stem_masks(rows, cols):
    row = lax.broadcasted_iota(jnp.int32, (rows, cols), 0)
    col = lax.broadcasted_iota(jnp.int32, (rows, cols), 1)
    group = (row % MEL) // PATCH
    first = group * CH
    return (col >= first) & (col < first + CH)


def tap_select(rows):
    row = lax.broadcasted_iota(jnp.int32, (rows, 16), 0)
    tap = lax.broadcasted_iota(jnp.int32, (rows, 16), 1)
    return (tap == PATCH * (row // MEL) + row % PATCH).astype(F32).astype(BF16)


def channel_select():
    row = lax.broadcasted_iota(jnp.int32, (CH, D), 0)
    col = lax.broadcasted_iota(jnp.int32, (CH, D), 1)
    return (col % CH == row).astype(F32).astype(BF16)


def stem_kernel(
    unused, frames_of, arrived, stem_weight, first_gain, conv_kernel, cotangent, ker,
    stem_total, embedded, normed, normed_t, frames_t, spectrum, mix_grad, wide, big,
):
    wide[...] = arrived[...].astype(F32)
    taps = mm(tap_select(TOK), stem_weight[...]).astype(BF16)
    spread = mm(taps, channel_select())
    big[...] = jnp.where(stem_masks(TOK, D), spread, 0.0).astype(BF16)
    padded = jnp.concatenate([conv_kernel[...], jnp.zeros((1, D), F32)], axis=0)
    spectrum[...] = mm(ker[...], thrice(padded))

    def one(u, carry):
        base = pl.multiple_of(u * UTT, UTT)
        rows = pl.ds(base, UTT)
        parts = [wide[pl.ds(base * PATCH + i, UTT, stride=PATCH), :].astype(BF16) for i in range(PATCH)]
        frames = jnp.concatenate(parts, axis=1)
        total = mm(frames, big[...])
        stem_total[rows, :] = total
        valid = keep(frames_of[u] // PATCH, (UTT, D))
        kept = jnp.where(valid, total * jax.nn.sigmoid(total), 0.0).astype(BF16)
        embedded[rows, :] = kept
        unit, scale = normalise(kept.astype(F32))
        narrow = (unit * first_gain[...]).astype(BF16)
        normed[rows, :] = narrow
        normed_t[:, rows] = narrow.T
        frames_t[:, rows] = frames.T
        mix_grad[rows, :] = jnp.where(valid, cotangent[rows, :].astype(F32), 0.0).astype(BF16)
        return carry

    lax.fori_loop(0, NU, one, 0)


def assemble(offsets, pieces, held, sems):
    copies = []
    for p, piece in enumerate(pieces):
        for j, (second, first) in enumerate(PIECES[p % len(PIECES)]):
            block = p // len(PIECES) * 16 + second * 4 + first
            start = pl.multiple_of(offsets[block], 16)
            copies.append(pltpu.make_async_copy(piece.at[j], held.at[pl.ds(start, ROWS), :], sems.at[block]))
    for copy in copies:
        copy.start()
    for copy in copies:
        copy.wait()


def gate_kernel(offsets, frames_of, *refs):
    pieces, refs = refs[:NP], refs[NP + 2 :]
    normed, spectrum, fwd, inv, value, gate, filtered, held, sems = refs
    n = pl.program_id(0)

    @pl.when(n == 0)
    def _():
        assemble(offsets, pieces, held, sems)

    start = pl.multiple_of(n * CB, CB)
    value[...] = mm(normed[...], held[:, pl.ds(start, CB)])
    gate[...] = mm(normed[...], held[:, pl.ds(pl.multiple_of(D + start, CB), CB)])
    re, im = spectrum[:IM, :], spectrum[IM:, :]
    for u in range(NU):
        rows = slice(u * UTT, (u + 1) * UTT)
        gated = value[rows, :] * jax.nn.sigmoid(gate[rows, :])
        gated = jnp.where(keep(frames_of[u] // PATCH, (UTT, CB)), gated, 0.0)
        seen = mm(fwd[...], twice(gated))
        a, b = seen[:IM], seen[IM:]
        moved = jnp.concatenate([a * re - b * im, a * im + b * re], axis=0)
        filtered[rows, :] = mm(inv[...], twice(moved))


def block_start(slots, i, flip):
    core = slots[32] if flip == 0 else 1 - slots[32]
    return pl.multiple_of((2 * i + core) * ROWS, 16)


def out_kernel(slots, unused, unused_too, filtered, mix_grad, second_gain, mine, other, swished, turned, term):
    def ahead(u, carry):
        rows = pl.ds(pl.multiple_of(u * UTT, UTT), UTT)
        unit, unused = normalise(filtered[rows, :])
        z = unit * second_gain[...]
        narrow = (z * jax.nn.sigmoid(z)).astype(BF16)
        swished[rows, :] = narrow
        turned[:, rows] = narrow.T
        return carry

    lax.fori_loop(0, NU, ahead, 0)

    def product(n, carry):
        cols = pl.ds(pl.multiple_of(n * CB, CB), CB)
        term[...] = mm(turned[...], mix_grad[:, cols]).astype(BF16)
        for i in range(16):
            mine[slots[i], :, cols] = term[pl.ds(block_start(slots, i, 0), ROWS), :]
            other[slots[16 + i], :, cols] = term[pl.ds(block_start(slots, i, 1), ROWS), :]
        return carry

    lax.fori_loop(0, NB, product, 0)


def mid_kernel(offsets, *refs):
    pieces, refs = refs[:NP], refs[NP:]
    filtered, mix_grad, second_gain, filter_grad, second_grad, held, sems, back = refs[3:]
    assemble(offsets, pieces, held, sems)
    second_grad[...] = jnp.zeros((1, D), F32)

    def product(n, carry):
        cols = pl.ds(pl.multiple_of(n * CB, CB), CB)
        back[:, cols] = mm_nt(mix_grad[...], held[cols, :])
        return carry

    lax.fori_loop(0, NB, product, 0)

    def behind(u, carry):
        rows = pl.ds(pl.multiple_of(u * UTT, UTT), UTT)
        unit, scale = normalise(filtered[rows, :])
        z = unit * second_gain[...]
        sig = jax.nn.sigmoid(z)
        dz = back[rows, :] * (sig * (1.0 + z * (1.0 - sig)))
        second_grad[...] += jnp.sum(dz * unit, axis=0, keepdims=True)
        filter_grad[rows, :] = normalise_back(dz * second_gain[...], unit, scale)
        return carry

    lax.fori_loop(0, NU, behind, 0)


def conv_back_kernel(
    slots, frames_of, unused_1, unused_2, unused_3, value, gate, filter_grad, normed_t, spectrum, fwd, inv_t, fwd_t, ker_t,
    value_grad, gate_grad, mine, other, conv_grad, term,
):
    re, im = spectrum[:IM, :], spectrum[IM:, :]
    sum_re = jnp.zeros((IM, CB), F32)
    sum_im = jnp.zeros((IM, CB), F32)
    for u in range(NU):
        rows = slice(u * UTT, (u + 1) * UTT)
        valid = keep(frames_of[u] // PATCH, (UTT, CB))
        v = value[rows, :]
        sig = jax.nn.sigmoid(gate[rows, :])
        gated = jnp.where(valid, v * sig, 0.0)
        seen = mm(fwd[...], twice(gated))
        a, b = seen[:IM], seen[IM:]
        grad = mm(inv_t[...], twice(filter_grad[rows, :]))
        da, db = grad[:IM], grad[IM:]
        sum_re = sum_re + a * da + b * db
        sum_im = sum_im + a * db - b * da
        spread = jnp.concatenate([re * da + im * db, re * db - im * da], axis=0)
        gated_grad = jnp.where(valid, mm(fwd_t[...], twice(spread)), 0.0)
        part = gated_grad * sig
        value_grad[rows, :] = part.astype(BF16)
        gate_grad[rows, :] = (part * v * (1.0 - sig)).astype(BF16)
    conv_grad[...] = mm(ker_t[...], thrice(jnp.concatenate([sum_re, sum_im], axis=0)))
    for h, grad_ref in enumerate((value_grad, gate_grad)):
        term[...] = mm(normed_t[...], grad_ref[...]).astype(BF16)
        for i in range(16):
            cols = slice(h * CB, (h + 1) * CB)
            mine[slots[i], :, cols] = term[pl.ds(block_start(slots, i, 0), ROWS), :]
            other[slots[16 + i], :, cols] = term[pl.ds(block_start(slots, i, 1), ROWS), :]


def stem_back_kernel(offsets, frames_of, *refs):
    pieces, refs = refs[:NP], refs[NP:]
    grads, refs = refs[:4], refs[4:]
    (unused_1, unused_2, unused_3, embedded, stem_total, mix_grad, first_gain, frames_t,
     first_grad, stem_grad, held, sems, back, pre_grad) = refs
    assemble(offsets, pieces, held, sems)
    first_grad[...] = jnp.zeros((1, D), F32)

    def product(n, carry):
        cols = pl.ds(pl.multiple_of(n * CB, CB), CB)
        total = jnp.zeros((TOK, CB), F32)
        begin = 0
        for grad in grads:
            total = total + mm_nt(grad[...], held[cols, begin : begin + grad.shape[1]])
            begin += grad.shape[1]
        back[:, cols] = total
        return carry

    lax.fori_loop(0, NB, product, 0)

    def behind(u, carry):
        rows = pl.ds(pl.multiple_of(u * UTT, UTT), UTT)
        unit, scale = normalise(embedded[rows, :].astype(F32))
        grad = back[rows, :]
        first_grad[...] += jnp.sum(grad * unit, axis=0, keepdims=True)
        grad = normalise_back(grad * first_gain[...], unit, scale) + mix_grad[rows, :].astype(F32)
        total = stem_total[rows, :]
        sig = jax.nn.sigmoid(total)
        grad = grad * (sig * (1.0 + total * (1.0 - sig)))
        valid = keep(frames_of[u] // PATCH, (UTT, D))
        pre_grad[rows, :] = jnp.where(valid, grad, 0.0).astype(BF16)
        return carry

    lax.fori_loop(0, NU, behind, 0)
    outer = mm(frames_t[...], pre_grad[...])
    outer = jnp.where(stem_masks(TOK, D), outer, 0.0)
    pick = tap_select(TOK).T
    folded = mm(jnp.concatenate([pick, pick], axis=1), split_rows(outer))
    channel = channel_select()
    high = folded.astype(BF16)
    low = (folded - high.astype(F32)).astype(BF16)
    stem_grad[...] = mm_nt(high, channel) + mm_nt(low, channel)


def split_rows(values):
    high = values.astype(BF16)
    low = (values - high.astype(F32)).astype(BF16)
    return jnp.concatenate([high, low], axis=0)


def mixed_kernel(offsets, frames_of, *refs):
    pieces, refs = refs[:NP], refs[NP:]
    unused, swished, embedded, output, held, sems = refs
    assemble(offsets, pieces, held, sems)

    def product(n, carry):
        cols = pl.ds(pl.multiple_of(n * CB, CB), CB)
        mixed = mm(swished[...], held[:, cols])
        for u in range(NU):
            rows = slice(u * UTT, (u + 1) * UTT)
            total = embedded[rows, cols].astype(F32) + mixed[rows]
            valid = keep(frames_of[u] // PATCH, (UTT, CB))
            output[rows, cols] = jnp.where(valid, total, 0.0).astype(BF16)
        return carry

    lax.fori_loop(0, NB, product, 0)


def chip_sum_kernel(mine_1, other_1, mine_2, other_2, *groups):
    wide = mine_1.shape[-1]
    for r, group in enumerate(groups):
        group[0, :, :wide] = (mine_1[r, 0].astype(F32) + other_1[r, 0].astype(F32)).astype(BF16)
        group[0, :, wide:] = (mine_2[r, 0].astype(F32) + other_2[r, 0].astype(F32)).astype(BF16)


SMEM = pl.BlockSpec(memory_space=pltpu.SMEM)
ANY = pl.BlockSpec(memory_space=pl.ANY)
VMEM = pl.BlockSpec(memory_space=pltpu.VMEM)


def shaped(shape, dtype):
    return jax.ShapeDtypeStruct(shape, dtype)


def call(kernel, name, operands, in_specs, outs, out_specs, scratch, flops, nbytes, vmem, grid=None):
    more = {} if grid is None else {"grid": grid}
    return pl.pallas_call(
        kernel,
        name=name,
        out_shape=outs,
        in_specs=in_specs,
        out_specs=out_specs,
        scratch_shapes=scratch,
        compiler_params=pltpu.CompilerParams(vmem_limit_bytes=vmem * MIB),
        cost_estimate=pl.CostEstimate(flops=flops // COST, bytes_accessed=nbytes // COST, transcendentals=0),
        **more,
    )(*operands)


def stem(before, arrived, frames_of, stem_weight, first_gain, conv_kernel, cotangent, tables):
    outs = [
        shaped((TOK, D), F32), shaped((TOK, D), BF16), shaped((TOK, D), BF16), shaped((D, TOK), BF16),
        shaped((TOK, TOK), BF16), shaped((SPEC, D), F32), shaped((TOK, D), BF16),
    ]
    return call(
        stem_kernel, "stem",
        (before, frames_of, arrived, stem_weight, first_gain, conv_kernel, cotangent, tables["ker"]),
        [ANY, SMEM] + [VMEM] * 6, outs, [VMEM] * 7,
        [pltpu.VMEM((TOK * PATCH, MEL), F32), pltpu.VMEM((TOK, D), BF16)],
        2 * TOK * TOK * D, 14 * MIB, 56,
    )


def gate_forward(offsets, frames_of, pieces, before, normed, spectrum, tables):
    whole = lambda n: (0, 0)
    block = lambda n: (0, n)
    return call(
        gate_kernel, "gate",
        (offsets, frames_of, *pieces, *before, normed, spectrum, tables["fwd"], tables["inv"]),
        [SMEM, SMEM] + [ANY] * (NP + 2)
        + [pl.BlockSpec((TOK, D), whole), pl.BlockSpec((SPEC, CB), block),
           pl.BlockSpec(tables["fwd"].shape, whole), pl.BlockSpec(tables["inv"].shape, whole)],
        [shaped((TOK, D), F32)] * 3, [pl.BlockSpec((TOK, CB), block)] * 3,
        [pltpu.VMEM((D, 2 * D), BF16), pltpu.SemaphoreType.DMA((32,))],
        2 * TOK * D * 2 * D, 22 * MIB, 56, grid=(NB,),
    )


def out_grad(slots, before, filtered, mix_grad, second_gain):
    half = shaped((16, ROWS, D), BF16)
    return call(
        out_kernel, "out_grad", (slots, *before, filtered, mix_grad, second_gain),
        [SMEM, ANY, ANY] + [VMEM] * 3, [half, half, shaped((TOK, D), BF16)], [VMEM] * 3,
        [pltpu.VMEM((D, TOK), BF16), pltpu.VMEM((D, CB), BF16)],
        2 * TOK * D * D, 11 * MIB, 56,
    )


def middle(offsets, pieces, before, filtered, mix_grad, second_gain):
    return call(
        mid_kernel, "middle", (offsets, *pieces, *before, filtered, mix_grad, second_gain),
        [SMEM] + [ANY] * (NP + 3) + [VMEM] * 3, [shaped((TOK, D), F32), shaped((1, D), F32)], [VMEM] * 2,
        [pltpu.VMEM((D, D), BF16), pltpu.SemaphoreType.DMA((32,)), pltpu.VMEM((TOK, D), F32)],
        2 * TOK * D * D, 13 * MIB, 56,
    )


def conv_back(slots, frames_of, before, value, gate, filter_grad, normed_t, spectrum, tables, begin, count):
    whole = lambda n: (0, 0)
    block = lambda n: (0, n + begin)
    own = lambda n: (0, n)
    width = count * CB
    names = ("fwd", "inv_t", "fwd_t", "ker_t")
    half = shaped((16, ROWS, 2 * width), BF16)
    half_spec = pl.BlockSpec((16, ROWS, 2 * CB), lambda n: (0, 0, n))
    outs = [shaped((TOK, width), BF16), shaped((TOK, width), BF16), half, half, shaped((32, width), F32)]
    return call(
        conv_back_kernel, "conv_back",
        (slots, frames_of, *before, value, gate, filter_grad, normed_t, spectrum, *[tables[k] for k in names]),
        [SMEM, SMEM, ANY, ANY, ANY] + [pl.BlockSpec((TOK, CB), block)] * 3
        + [pl.BlockSpec((D, TOK), whole), pl.BlockSpec((SPEC, CB), block)]
        + [pl.BlockSpec(tables[k].shape, whole) for k in names],
        outs,
        [pl.BlockSpec((TOK, CB), own)] * 2 + [half_spec, half_spec, pl.BlockSpec((32, CB), own)],
        [pltpu.VMEM((D, CB), BF16)], 2 * TOK * D * width * 2, 22 * MIB * count // NB, 56, grid=(count,),
    )


def stem_back(offsets, frames_of, pieces, grads, before, embedded, stem_total, mix_grad, first_gain, frames_t):
    return call(
        stem_back_kernel, "stem_back",
        (offsets, frames_of, *pieces, *grads, *before, embedded, stem_total, mix_grad, first_gain, frames_t),
        [SMEM, SMEM] + [ANY] * NP + [VMEM] * 4 + [ANY] * 3 + [VMEM] * 5,
        [shaped((1, D), F32), shaped((16, CH), F32)], [VMEM] * 2,
        [pltpu.VMEM((D, 2 * D), BF16), pltpu.SemaphoreType.DMA((32,)), pltpu.VMEM((TOK, D), F32), pltpu.VMEM((TOK, D), BF16)],
        2 * TOK * D * 2 * D, 20 * MIB, 56,
    )


def mixed_out(offsets, frames_of, pieces, before, swished, embedded):
    return call(
        mixed_kernel, "mixed",
        (offsets, frames_of, *pieces, before, swished, embedded),
        [SMEM, SMEM] + [ANY] * (NP + 1) + [VMEM] * 2,
        shaped((TOK, D), BF16), VMEM,
        [pltpu.VMEM((D, D), BF16), pltpu.SemaphoreType.DMA((32,))],
        2 * TOK * D * D, 10 * MIB, 56,
    )


def chip_sums(parts):
    operands = [value.reshape(4, 4, *value.shape[1:]) for part in parts for value in part]
    width = 2 * D
    spec = lambda value: pl.BlockSpec((4, 1, *value.shape[2:]), lambda m: (0, m, 0, 0))
    return call(
        chip_sum_kernel, "chip_sum", operands, [spec(value) for value in operands],
        [shaped((4, ROWS, width), BF16)] * 4, [pl.BlockSpec((1, ROWS, width), lambda m: (m, 0, 0))] * 4,
        [], 16 * ROWS * width, 14 * MIB, 48, grid=(4,),
    )


def place(x, y, z, c):
    return ((x % 4 * 4 + y % 4) * 4 + z % 4) * 2 + c


def pairs(step):
    found = []
    for x in range(4):
        for y in range(4):
            for z in range(4):
                for c in range(2):
                    found.append((place(x, y, z, c), step(x, y, z, c)))
    return found


def along_first(r):
    return pairs(lambda x, y, z, c: place(x, y ^ (r * c), z ^ (r * (1 - c)), c))


def along_second(r):
    return pairs(lambda x, y, z, c: place(x, y ^ (r * (1 - c)), z ^ (r * c), c))


def along_x(r):
    return pairs(lambda x, y, z, c: place(x ^ r, y, z, c))


def other_core():
    return pairs(lambda x, y, z, c: place(x, y, z, 1 - c))


def send(values, where):
    return lax.ppermute(values, ALL, where)


def gather_offsets(y, z, c):
    m, j = np.divmod(np.arange(16, dtype=np.int32), 4)

    def of(core):
        row_y = y ^ jnp.where(core == 0, m, j)
        row_z = z ^ jnp.where(core == 0, j, m)
        return ((row_y * 4 + row_z) * 2 + core) * ROWS

    return jnp.concatenate([of(c), of(1 - c)]).astype(jnp.int32)


def scatter_slots(y, z, c):
    block = np.arange(16, dtype=np.int32)
    far_y, far_z = (block // 4) ^ y, (block % 4) ^ z

    def of(core):
        return jnp.where(core == 0, far_z * 4 + far_y, far_y * 4 + far_z)

    return jnp.concatenate([of(c), of(1 - c), c[None]]).astype(jnp.int32)


def zero_of(values):
    return values[(0,) * values.ndim] * 0


def gather_near(shards):
    joined = jnp.concatenate(shards, axis=1)
    near = [joined] + [send(joined, along_first(r)) for r in (1, 2, 3)]
    wide = shards[0].shape[1]
    return jnp.stack([block[:, :wide] for block in near]), jnp.stack([block[:, wide:] for block in near])


def gather_far(near):
    halves = near[:2], near[2:]
    first = [send(half, along_second(r)) for half, r in zip(halves, (1, 3))]
    second = [
        send(jnp.stack([half, got]), along_second(r)) for half, got, r in zip(halves, first, (3, 1))
    ]
    return first, second


def gather_pieces(near, first, second, after):
    own = [near, first[0], first[1], second[0].reshape(4, *near.shape[1:]), second[1].reshape(4, *near.shape[1:])]
    return own + [send(piece + after, other_core()) for piece in own]


PIECES = (
    ((0, 0), (0, 1), (0, 2), (0, 3)),
    ((1, 0), (1, 1)),
    ((3, 2), (3, 3)),
    ((3, 0), (3, 1), (2, 0), (2, 1)),
    ((1, 2), (1, 3), (2, 2), (2, 3)),
)
NP = 2 * len(PIECES)


def total_of(parts):
    summed = parts[0].astype(F32)
    for part in parts[1:]:
        summed = summed + part.astype(F32)
    return summed


def chip_sum(mine, other):
    other = send(other, other_core())
    return [total_of([mine[4 * j : 4 * j + 4], other[4 * j : 4 * j + 4]]).astype(BF16) for j in range(4)]


def scatter_first(groups):
    return [groups[0]] + [send(groups[r], along_first(r)) for r in (1, 2, 3)]


def scatter_rest(near):
    close = total_of([near[0]] + [send(near[r], along_second(r)) for r in (1, 2, 3)]).astype(BF16)
    wide = close.shape[1] // 2
    halves = []
    for half, order in ((close[:, :wide], (1, 3)), (close[:, wide:], (3, 1))):
        half = total_of([half, send(half, along_x(order[0]))]).astype(BF16)
        halves.append(total_of([half, send(half, along_x(order[1]))]))
    return jnp.concatenate(halves, axis=1)


def half_of_chip(values, c):
    return jnp.where(c == 0, values[0], values[1]) + send(jnp.where(c == 0, values[1], values[0]), other_core())


def finish_small(values, rows, c):
    values = total_of([values] + [send(values, along_first(r)) for r in (1, 2, 3)])
    other = send(values, other_core())
    mine, late = values[:rows], values[rows:] + other[rows:]
    other = other[:rows]
    return jnp.concatenate([jnp.where(c == 0, mine, other), jnp.where(c == 0, other, mine)]), late


def body(
    tables, log_mel, bucket_list, utterance_frames, stem_weight, first_gain, gate_proj, conv_kernel, second_gain,
    out_proj, cotangent,
):
    y, z, c = lax.axis_index("y"), lax.axis_index("z"), lax.axis_index("c")
    offsets = gather_offsets(y, z, c)
    slots = scatter_slots(y, z, c)
    tables = {name: jnp.asarray(value) for name, value in tables.items()}
    first_gain, second_gain = first_gain[None], second_gain[None]

    gate_near, out_near = gather_near((gate_proj, out_proj))
    outgoing = jnp.take(log_mel, bucket_list[0], axis=0) + zero_of(gate_near)
    arrived = lax.all_to_all(outgoing, ALL, split_axis=0, concat_axis=0, tiled=True)
    gate_far = gather_far(gate_near)
    stem_total, embedded, normed, normed_t, frames_t, spectrum, mix_grad = stem(
        gate_far[0][0], arrived.reshape(TOK * PATCH, MEL), utterance_frames, stem_weight, first_gain, conv_kernel, cotangent, tables
    )
    gate_pieces = gather_pieces(gate_near, *gate_far, zero_of(normed))
    out_near = out_near + sum(zero_of(piece) for piece in gate_far[1])
    out_far = gather_far(out_near)
    out_pieces = gather_pieces(out_near, *out_far, jnp.zeros((), BF16))
    value, gate, filtered = gate_forward(
        offsets, utterance_frames, gate_pieces, out_far[0], normed, spectrum, tables
    )
    out_mine, out_other, swished = out_grad(slots, out_far[1], filtered, mix_grad, second_gain)
    out_groups = chip_sum(out_mine, out_other)
    filter_grad, second_grad = middle(offsets, out_pieces, out_groups[1:], filtered, mix_grad, second_gain)
    out_groups = scatter_first(out_groups)
    grads, nears, convs = [], [], []
    for begin, count in ((0, 4), (4, 2)):
        value_grad, gate_grad, mine, other, conv_grad = conv_back(
            slots, utterance_frames, out_groups[1:], value, gate, filter_grad, normed_t, spectrum, tables, begin, count
        )
        grads.append((value_grad, gate_grad))
        nears.append((mine, send(other, other_core())))
        convs.append(conv_grad[:TAPS])
    gate_groups = chip_sums(nears)
    first_grad, stem_grad = stem_back(
        offsets, utterance_frames, gate_pieces, [pair[k] for k in range(2) for pair in grads], gate_groups[1:], embedded,
        stem_total, mix_grad, first_gain, frames_t,
    )
    output = mixed_out(offsets, utterance_frames, out_pieces, first_grad, swished, embedded)
    early = jnp.concatenate([jnp.concatenate(convs, axis=1), second_grad], axis=0)
    early = half_of_chip(early.reshape(2, 16, D), c)
    follow = zero_of(output).astype(F32) + zero_of(first_grad)
    terms = [scatter_first(gate_groups), out_groups]
    near = jnp.concatenate([(total_of(term) + follow).astype(BF16) for term in terms], axis=-1)
    late = jnp.concatenate([first_grad, jnp.pad(stem_grad.reshape(1, -1), ((0, 0), (0, D - 16 * CH)))], axis=0)
    small = jnp.concatenate([early, late, jnp.zeros((6, D), F32)], axis=0)
    small = jnp.concatenate([small[:8], small[8:16], small[16:]], axis=1).astype(BF16)
    near = jnp.concatenate([near, jnp.broadcast_to(small[None], (4, *small.shape))], axis=1)
    sums = scatter_rest(near)
    small = sums[ROWS:]
    early, late = finish_small(
        jnp.concatenate([small[:, :D], small[:, D : 2 * D], small[:2, 2 * D :]]), 16, c
    )
    sums = sums[:ROWS]
    blocks = [sums[:, i * CB : (i + 1) * CB] for i in range(2 * NB)]
    gate_sums = jnp.concatenate(blocks[::2] + blocks[1::2], axis=1)
    return (
        output, gate_sums, sums[:, 2 * D :], late[1, : 16 * CH].reshape(16, CH), late[0],
        early[:TAPS], early[TAPS],
    )


def solution(mesh):
    grid = Mesh(mesh.devices.reshape(4, 4, 4, 2), ALL)
    rows = ("y", "z", "c")
    return jax.shard_map(
        functools.partial(body, transforms()),
        mesh=grid,
        in_specs=(
            P(ALL, None, None), P(ALL, None), P(ALL), P(), P(), P(rows, None), P(), P(), P(rows, None), P(ALL, None),
        ),
        out_specs=(P(ALL, None), P(rows, None), P(rows, None), P(), P(), P(), P()),
        check_vma=False,
    )
```

```python
import functools

import jax
import jax.numpy as jnp
import numpy as np
from jax import lax
from jax.experimental import pallas as pl
from jax.experimental.pallas import tpu as pltpu
from jax.sharding import Mesh
from jax.sharding import PartitionSpec as P

PATCH = 4
UTT = 128
TOK = 512
NU = TOK // UTT
D = 1536
MEL = 128
CH = 48
TAPS = 31
HALF = TAPS // 2
EPS = 1e-05
ROWS = 48
CB = 256
NB = D // CB
ALL = ("x", "y", "z", "c")
F32 = jnp.float32
BF16 = jnp.bfloat16
MIB = 1024 * 1024
COST = 1

CYC = 144
BINS = CYC // 2 + 1
IM = 80
SPEC = 160


def hi_lo(values):
    high = values.astype(np.float32).astype(jnp.bfloat16)
    low = (values - high.astype(np.float64)).astype(np.float32).astype(jnp.bfloat16)
    return high, low


def side_by_side(values, three=False):
    high, low = hi_lo(values)
    parts = [high, low] + ([high] if three else [])
    return np.concatenate(parts, axis=1)


def transforms():
    angle = 2 * np.pi / CYC
    bins = np.arange(BINS)[:, None]
    places = np.arange(UTT)[None, :]
    offsets = np.arange(TAPS)[None, :] - HALF
    forward = np.zeros((SPEC, UTT))
    forward[:BINS] = np.cos(angle * bins * places)
    forward[IM : IM + BINS] = -np.sin(angle * bins * places)
    kernel = np.zeros((SPEC, 32))
    kernel[:BINS, :TAPS] = np.cos(angle * bins * offsets)
    kernel[IM : IM + BINS, :TAPS] = np.sin(angle * bins * offsets)
    weight = np.full((BINS, 1), 2.0 / CYC)
    weight[0] = weight[-1] = 1.0 / CYC
    back = np.zeros((UTT, SPEC))
    back[:, :BINS] = (weight * np.cos(angle * bins * places)).T
    back[:, IM : IM + BINS] = -(weight * np.sin(angle * bins * places)).T
    return {
        "fwd": side_by_side(forward),
        "inv": side_by_side(back),
        "fwd_t": side_by_side(forward.T),
        "inv_t": side_by_side(back.T),
        "ker": side_by_side(kernel, True),
        "ker_t": side_by_side(kernel.T, True),
    }


def twice(values):
    narrow = values.astype(BF16)
    return jnp.concatenate([narrow, narrow], axis=0)


def thrice(values):
    high = values.astype(BF16)
    low = (values - high.astype(F32)).astype(BF16)
    return jnp.concatenate([high, high, low], axis=0)


def mm(left, right):
    return jnp.dot(left, right, preferred_element_type=F32)


def mm_nt(left, right):
    return lax.dot_general(left, right, (((1,), (1,)), ((), ())), preferred_element_type=F32)


def keep(limit, shape):
    return lax.broadcasted_iota(jnp.int32, shape, 0) < limit


def row_mean(values):
    return jnp.sum(values, axis=-1, keepdims=True) * (1.0 / D)


def normalise(values):
    centred = values - row_mean(values)
    scale = lax.rsqrt(row_mean(centred * centred) + EPS)
    return centred * scale, scale


def normalise_back(grad, unit, scale):
    return scale * (grad - row_mean(grad) - unit * row_mean(grad * unit))


def stem_masks(rows, cols):
    row = lax.broadcasted_iota(jnp.int32, (rows, cols), 0)
    col = lax.broadcasted_iota(jnp.int32, (rows, cols), 1)
    group = (row % MEL) // PATCH
    first = group * CH
    return (col >= first) & (col < first + CH)


def tap_select(rows):
    row = lax.broadcasted_iota(jnp.int32, (rows, 16), 0)
    tap = lax.broadcasted_iota(jnp.int32, (rows, 16), 1)
    return (tap == PATCH * (row // MEL) + row % PATCH).astype(F32).astype(BF16)


def channel_select():
    row = lax.broadcasted_iota(jnp.int32, (CH, D), 0)
    col = lax.broadcasted_iota(jnp.int32, (CH, D), 1)
    return (col % CH == row).astype(F32).astype(BF16)


def stem_kernel(
    unused, frames_of, arrived, stem_weight, first_gain, conv_kernel, cotangent, ker,
    stem_total, embedded, normed, normed_t, frames_t, spectrum, mix_grad, wide, big,
):
    wide[...] = arrived[...].astype(F32)
    taps = mm(tap_select(TOK), stem_weight[...]).astype(BF16)
    spread = mm(taps, channel_select())
    big[...] = jnp.where(stem_masks(TOK, D), spread, 0.0).astype(BF16)
    padded = jnp.concatenate([conv_kernel[...], jnp.zeros((1, D), F32)], axis=0)
    spectrum[...] = mm(ker[...], thrice(padded))

    def one(u, carry):
        base = pl.multiple_of(u * UTT, UTT)
        rows = pl.ds(base, UTT)
        parts = [wide[pl.ds(base * PATCH + i, UTT, stride=PATCH), :].astype(BF16) for i in range(PATCH)]
        frames = jnp.concatenate(parts, axis=1)
        total = mm(frames, big[...])
        stem_total[rows, :] = total
        valid = keep(frames_of[u] // PATCH, (UTT, D))
        kept = jnp.where(valid, total * jax.nn.sigmoid(total), 0.0).astype(BF16)
        embedded[rows, :] = kept
        unit, scale = normalise(kept.astype(F32))
        narrow = (unit * first_gain[...]).astype(BF16)
        normed[rows, :] = narrow
        normed_t[:, rows] = narrow.T
        frames_t[:, rows] = frames.T
        mix_grad[rows, :] = jnp.where(valid, cotangent[rows, :].astype(F32), 0.0).astype(BF16)
        return carry

    lax.fori_loop(0, NU, one, 0)


def assembly(offsets, pieces, held, sems):
    copies = []
    layout = PIECES if len(pieces) == NP else DIRECT
    for p, piece in enumerate(pieces):
        for j, (second, first) in enumerate(layout[p % len(layout)]):
            block = p // len(layout) * 16 + second * 4 + first
            start = pl.multiple_of(offsets[block], 16)
            copies.append(pltpu.make_async_copy(piece.at[j], held.at[pl.ds(start, ROWS), :], sems.at[block]))
    return copies


def assemble(offsets, pieces, held, sems):
    copies = assembly(offsets, pieces, held, sems)
    for copy in copies:
        copy.start()
    for copy in copies:
        copy.wait()


def gate_kernel(offsets, frames_of, *refs):
    pieces, refs = refs[:NP], refs[NP:]
    normed, spectrum, fwd, inv, value, gate, filtered, held, sems = refs
    n = pl.program_id(0)

    @pl.when(n == 0)
    def _():
        assemble(offsets, pieces, held, sems)

    start = pl.multiple_of(n * CB, CB)
    value[...] = mm(normed[...], held[:, pl.ds(start, CB)])
    gate[...] = mm(normed[...], held[:, pl.ds(pl.multiple_of(D + start, CB), CB)])
    re, im = spectrum[:IM, :], spectrum[IM:, :]
    for u in range(NU):
        rows = slice(u * UTT, (u + 1) * UTT)
        gated = value[rows, :] * jax.nn.sigmoid(gate[rows, :])
        gated = jnp.where(keep(frames_of[u] // PATCH, (UTT, CB)), gated, 0.0)
        seen = mm(fwd[...], twice(gated))
        a, b = seen[:IM], seen[IM:]
        moved = jnp.concatenate([a * re - b * im, a * im + b * re], axis=0)
        filtered[rows, :] = mm(inv[...], twice(moved))


def block_start(slots, i, flip):
    core = slots[32] if flip == 0 else 1 - slots[32]
    return pl.multiple_of((2 * i + core) * ROWS, 16)


def out_kernel(slots, unused_1, unused_2, unused_3, filtered, mix_grad, second_gain, mine, other, swished, turned, term):
    def ahead(u, carry):
        rows = pl.ds(pl.multiple_of(u * UTT, UTT), UTT)
        unit, unused = normalise(filtered[rows, :])
        z = unit * second_gain[...]
        narrow = (z * jax.nn.sigmoid(z)).astype(BF16)
        swished[rows, :] = narrow
        turned[:, rows] = narrow.T
        return carry

    lax.fori_loop(0, NU, ahead, 0)

    def product(n, carry):
        cols = pl.ds(pl.multiple_of(n * CB, CB), CB)
        term[...] = mm(turned[...], mix_grad[:, cols]).astype(BF16)
        for i in range(16):
            mine[slots[i], :, cols] = term[pl.ds(block_start(slots, i, 0), ROWS), :]
            other[slots[16 + i], :, cols] = term[pl.ds(block_start(slots, i, 1), ROWS), :]
        return carry

    lax.fori_loop(0, NB, product, 0)


def mid_kernel(offsets, *refs):
    pieces, refs = refs[:ND], refs[ND:]
    filtered, mix_grad, second_gain, filter_grad, second_grad, held, sems, back, slope, scales = refs
    copies = assembly(offsets, pieces, held, sems)
    for copy in copies:
        copy.start()
    second_grad[...] = jnp.zeros((1, D), F32)

    def ahead(u, carry):
        rows = pl.ds(pl.multiple_of(u * UTT, UTT), UTT)
        unit, scale = normalise(filtered[rows, :])
        z = unit * second_gain[...]
        sig = jax.nn.sigmoid(z)
        slope[rows, :] = sig * (1.0 + z * (1.0 - sig))
        filter_grad[rows, :] = unit
        scales[rows, :] = jnp.broadcast_to(scale, (UTT, 128))
        return carry

    lax.fori_loop(0, NU, ahead, 0)
    for copy in copies:
        copy.wait()

    def product(n, carry):
        cols = pl.ds(pl.multiple_of(n * 2 * CB, 2 * CB), 2 * CB)
        back[:, cols] = mm_nt(mix_grad[...], held[cols, :])
        return carry

    lax.fori_loop(0, NB // 2, product, 0)

    def behind(u, carry):
        rows = pl.ds(pl.multiple_of(u * UTT, UTT), UTT)
        unit = filter_grad[rows, :]
        dz = back[rows, :] * slope[rows, :]
        second_grad[...] += jnp.sum(dz * unit, axis=0, keepdims=True)
        filter_grad[rows, :] = normalise_back(dz * second_gain[...], unit, scales[rows, :1])
        return carry

    lax.fori_loop(0, NU, behind, 0)


def conv_back_kernel(
    slots, frames_of, unused_1, unused_2, unused_3, value, gate, filter_grad, normed_t, spectrum, fwd, inv_t, fwd_t, ker_t,
    value_grad, gate_grad, mine, other, conv_grad, term,
):
    re, im = spectrum[:IM, :], spectrum[IM:, :]
    sum_re = jnp.zeros((IM, CB), F32)
    sum_im = jnp.zeros((IM, CB), F32)
    for u in range(NU):
        rows = slice(u * UTT, (u + 1) * UTT)
        valid = keep(frames_of[u] // PATCH, (UTT, CB))
        v = value[rows, :]
        sig = jax.nn.sigmoid(gate[rows, :])
        gated = jnp.where(valid, v * sig, 0.0)
        seen = mm(fwd[...], twice(gated))
        a, b = seen[:IM], seen[IM:]
        grad = mm(inv_t[...], twice(filter_grad[rows, :]))
        da, db = grad[:IM], grad[IM:]
        sum_re = sum_re + a * da + b * db
        sum_im = sum_im + a * db - b * da
        spread = jnp.concatenate([re * da + im * db, re * db - im * da], axis=0)
        gated_grad = jnp.where(valid, mm(fwd_t[...], twice(spread)), 0.0)
        part = gated_grad * sig
        value_grad[rows, :] = part.astype(BF16)
        gate_grad[rows, :] = (part * v * (1.0 - sig)).astype(BF16)
    conv_grad[...] = mm(ker_t[...], thrice(jnp.concatenate([sum_re, sum_im], axis=0)))
    for h, grad_ref in enumerate((value_grad, gate_grad)):
        term[...] = mm(normed_t[...], grad_ref[...]).astype(BF16)
        for i in range(16):
            cols = slice(h * CB, (h + 1) * CB)
            mine[slots[i], :, cols] = term[pl.ds(block_start(slots, i, 0), ROWS), :]
            other[slots[16 + i], :, cols] = term[pl.ds(block_start(slots, i, 1), ROWS), :]


def stem_back_kernel(offsets, frames_of, *refs):
    pieces, refs = refs[:NP], refs[NP:]
    grads, refs = refs[:4], refs[4:]
    (unused_1, unused_2, unused_3, embedded, stem_total, mix_grad, first_gain, frames_t,
     first_grad, stem_grad, held, sems, back, pre_grad) = refs
    assemble(offsets, pieces, held, sems)
    first_grad[...] = jnp.zeros((1, D), F32)

    def product(n, carry):
        cols = pl.ds(pl.multiple_of(n * CB, CB), CB)
        total = jnp.zeros((TOK, CB), F32)
        begin = 0
        for grad in grads:
            total = total + mm_nt(grad[...], held[cols, begin : begin + grad.shape[1]])
            begin += grad.shape[1]
        back[:, cols] = total
        return carry

    lax.fori_loop(0, NB, product, 0)

    def behind(u, carry):
        rows = pl.ds(pl.multiple_of(u * UTT, UTT), UTT)
        unit, scale = normalise(embedded[rows, :].astype(F32))
        grad = back[rows, :]
        first_grad[...] += jnp.sum(grad * unit, axis=0, keepdims=True)
        grad = normalise_back(grad * first_gain[...], unit, scale) + mix_grad[rows, :].astype(F32)
        total = stem_total[rows, :]
        sig = jax.nn.sigmoid(total)
        grad = grad * (sig * (1.0 + total * (1.0 - sig)))
        valid = keep(frames_of[u] // PATCH, (UTT, D))
        pre_grad[rows, :] = jnp.where(valid, grad, 0.0).astype(BF16)
        return carry

    lax.fori_loop(0, NU, behind, 0)
    outer = mm(frames_t[...], pre_grad[...])
    outer = jnp.where(stem_masks(TOK, D), outer, 0.0)
    pick = tap_select(TOK).T
    folded = mm(jnp.concatenate([pick, pick], axis=1), split_rows(outer))
    channel = channel_select()
    high = folded.astype(BF16)
    low = (folded - high.astype(F32)).astype(BF16)
    stem_grad[...] = mm_nt(high, channel) + mm_nt(low, channel)


def split_rows(values):
    high = values.astype(BF16)
    low = (values - high.astype(F32)).astype(BF16)
    return jnp.concatenate([high, low], axis=0)


def mixed_kernel(offsets, frames_of, *refs):
    pieces, refs = refs[:ND], refs[ND:]
    unused, swished, embedded, output, held, sems = refs
    assemble(offsets, pieces, held, sems)

    def product(n, carry):
        cols = pl.ds(pl.multiple_of(n * CB, CB), CB)
        mixed = mm(swished[...], held[:, cols])
        for u in range(NU):
            rows = slice(u * UTT, (u + 1) * UTT)
            total = embedded[rows, cols].astype(F32) + mixed[rows]
            valid = keep(frames_of[u] // PATCH, (UTT, CB))
            output[rows, cols] = jnp.where(valid, total, 0.0).astype(BF16)
        return carry

    lax.fori_loop(0, NB, product, 0)


def chip_sum_kernel(mine_1, other_1, mine_2, other_2, *groups):
    wide = mine_1.shape[-1]
    for r, group in enumerate(groups):
        group[0, :, :wide] = (mine_1[r, 0].astype(F32) + other_1[r, 0].astype(F32)).astype(BF16)
        group[0, :, wide:] = (mine_2[r, 0].astype(F32) + other_2[r, 0].astype(F32)).astype(BF16)


SMEM = pl.BlockSpec(memory_space=pltpu.SMEM)
ANY = pl.BlockSpec(memory_space=pl.ANY)
VMEM = pl.BlockSpec(memory_space=pltpu.VMEM)


def shaped(shape, dtype):
    return jax.ShapeDtypeStruct(shape, dtype)


def call(kernel, name, operands, in_specs, outs, out_specs, scratch, flops, nbytes, vmem, grid=None):
    more = {} if grid is None else {"grid": grid}
    return pl.pallas_call(
        kernel,
        name=name,
        out_shape=outs,
        in_specs=in_specs,
        out_specs=out_specs,
        scratch_shapes=scratch,
        compiler_params=pltpu.CompilerParams(vmem_limit_bytes=vmem * MIB),
        cost_estimate=pl.CostEstimate(flops=flops // COST, bytes_accessed=nbytes // COST, transcendentals=0),
        **more,
    )(*operands)


def stem(before, arrived, frames_of, stem_weight, first_gain, conv_kernel, cotangent, tables):
    outs = [
        shaped((TOK, D), F32), shaped((TOK, D), BF16), shaped((TOK, D), BF16), shaped((D, TOK), BF16),
        shaped((TOK, TOK), BF16), shaped((SPEC, D), F32), shaped((TOK, D), BF16),
    ]
    return call(
        stem_kernel, "stem",
        (before, frames_of, arrived, stem_weight, first_gain, conv_kernel, cotangent, tables["ker"]),
        [ANY, SMEM] + [VMEM] * 6, outs, [VMEM] * 7,
        [pltpu.VMEM((TOK * PATCH, MEL), F32), pltpu.VMEM((TOK, D), BF16)],
        2 * TOK * TOK * D, 14 * MIB, 26,
    )


def gate_forward(offsets, frames_of, pieces, normed, spectrum, tables):
    whole = lambda n: (0, 0)
    block = lambda n: (0, n)
    return call(
        gate_kernel, "gate",
        (offsets, frames_of, *pieces, normed, spectrum, tables["fwd"], tables["inv"]),
        [SMEM, SMEM] + [ANY] * NP
        + [pl.BlockSpec((TOK, D), whole), pl.BlockSpec((SPEC, CB), block),
           pl.BlockSpec(tables["fwd"].shape, whole), pl.BlockSpec(tables["inv"].shape, whole)],
        [shaped((TOK, D), F32)] * 3, [pl.BlockSpec((TOK, CB), block)] * 3,
        [pltpu.VMEM((D, 2 * D), BF16), pltpu.SemaphoreType.DMA((32,))],
        2 * TOK * D * 2 * D, 22 * MIB, 26, grid=(NB,),
    )


def out_grad(slots, before, filtered, mix_grad, second_gain):
    half = shaped((16, ROWS, D), BF16)
    return call(
        out_kernel, "out_grad", (slots, *before, filtered, mix_grad, second_gain),
        [SMEM] + [ANY] * 3 + [VMEM] * 3, [half, half, shaped((TOK, D), BF16)], [VMEM] * 3,
        [pltpu.VMEM((D, TOK), BF16), pltpu.VMEM((D, CB), BF16)],
        16 * 2 * TOK * D * D, 16 * 11 * MIB, 24,
    )


def middle(offsets, pieces, filtered, mix_grad, second_gain):
    return call(
        mid_kernel, "middle", (offsets, *pieces, filtered, mix_grad, second_gain),
        [SMEM] + [ANY] * ND + [VMEM] * 3, [shaped((TOK, D), F32), shaped((1, D), F32)], [VMEM] * 2,
        [pltpu.VMEM((D, D), BF16), pltpu.SemaphoreType.DMA((32,)), pltpu.VMEM((TOK, D), F32),
         pltpu.VMEM((TOK, D), F32), pltpu.VMEM((TOK, 128), F32)],
        16 * 2 * TOK * D * D, 16 * 13 * MIB, 28,
    )


def conv_back(slots, frames_of, before, value, gate, filter_grad, normed_t, spectrum, tables, begin, count):
    whole = lambda n: (0, 0)
    block = lambda n: (0, n + begin)
    own = lambda n: (0, n)
    width = count * CB
    names = ("fwd", "inv_t", "fwd_t", "ker_t")
    half = shaped((16, ROWS, 2 * width), BF16)
    half_spec = pl.BlockSpec((16, ROWS, 2 * CB), lambda n: (0, 0, n))
    outs = [shaped((TOK, width), BF16), shaped((TOK, width), BF16), half, half, shaped((32, width), F32)]
    return call(
        conv_back_kernel, "conv_back",
        (slots, frames_of, *before, value, gate, filter_grad, normed_t, spectrum, *[tables[k] for k in names]),
        [SMEM, SMEM, ANY, ANY, ANY] + [pl.BlockSpec((TOK, CB), block)] * 3
        + [pl.BlockSpec((D, TOK), whole), pl.BlockSpec((SPEC, CB), block)]
        + [pl.BlockSpec(tables[k].shape, whole) for k in names],
        outs,
        [pl.BlockSpec((TOK, CB), own)] * 2 + [half_spec, half_spec, pl.BlockSpec((32, CB), own)],
        [pltpu.VMEM((D, CB), BF16)], 2 * TOK * D * width * 2 * 16, 22 * MIB * count // NB * 16, 22, grid=(count,),
    )


def stem_back(offsets, frames_of, pieces, grads, before, embedded, stem_total, mix_grad, first_gain, frames_t):
    return call(
        stem_back_kernel, "stem_back",
        (offsets, frames_of, *pieces, *grads, *before, embedded, stem_total, mix_grad, first_gain, frames_t),
        [SMEM, SMEM] + [ANY] * NP + [VMEM] * 4 + [ANY] * 3 + [VMEM] * 5,
        [shaped((1, D), F32), shaped((16, CH), F32)], [VMEM] * 2,
        [pltpu.VMEM((D, 2 * D), BF16), pltpu.SemaphoreType.DMA((32,)), pltpu.VMEM((TOK, D), F32), pltpu.VMEM((TOK, D), BF16)],
        16 * 2 * TOK * D * 2 * D, 16 * 20 * MIB, 36,
    )


def mixed_out(offsets, frames_of, pieces, before, swished, embedded):
    return call(
        mixed_kernel, "mixed",
        (offsets, frames_of, *pieces, before, swished, embedded),
        [SMEM, SMEM] + [ANY] * (ND + 1) + [VMEM] * 2,
        shaped((TOK, D), BF16), VMEM,
        [pltpu.VMEM((D, D), BF16), pltpu.SemaphoreType.DMA((32,))],
        2 * TOK * D * D, 10 * MIB, 18,
    )


def chip_sums(parts):
    operands = [value.reshape(4, 4, *value.shape[1:]) for part in parts for value in part]
    width = 2 * D
    spec = lambda value: pl.BlockSpec((4, 1, *value.shape[2:]), lambda m: (0, m, 0, 0))
    return call(
        chip_sum_kernel, "chip_sum", operands, [spec(value) for value in operands],
        [shaped((4, ROWS, width), BF16)] * 4, [pl.BlockSpec((1, ROWS, width), lambda m: (m, 0, 0))] * 4,
        [], 16 * ROWS * width, 14 * MIB, 18, grid=(4,),
    )


def place(x, y, z, c):
    return ((x % 4 * 4 + y % 4) * 4 + z % 4) * 2 + c


def pairs(step):
    found = []
    for x in range(4):
        for y in range(4):
            for z in range(4):
                for c in range(2):
                    found.append((place(x, y, z, c), step(x, y, z, c)))
    return found


def along_first(r):
    return pairs(lambda x, y, z, c: place(x, y ^ (r * c), z ^ (r * (1 - c)), c))


def along_second(r):
    return pairs(lambda x, y, z, c: place(x, y ^ (r * (1 - c)), z ^ (r * c), c))


def along_x(r):
    return pairs(lambda x, y, z, c: place(x ^ r, y, z, c))


def other_core():
    return pairs(lambda x, y, z, c: place(x, y, z, 1 - c))


def send(values, where):
    return lax.ppermute(values, ALL, where)


def gather_offsets(y, z, c):
    m, j = np.divmod(np.arange(16, dtype=np.int32), 4)

    def of(core):
        row_y = y ^ jnp.where(core == 0, m, j)
        row_z = z ^ jnp.where(core == 0, j, m)
        return ((row_y * 4 + row_z) * 2 + core) * ROWS

    return jnp.concatenate([of(c), of(1 - c)]).astype(jnp.int32)


def scatter_slots(y, z, c):
    block = np.arange(16, dtype=np.int32)
    far_y, far_z = (block // 4) ^ y, (block % 4) ^ z

    def of(core):
        return jnp.where(core == 0, far_z * 4 + far_y, far_y * 4 + far_z)

    return jnp.concatenate([of(c), of(1 - c), c[None]]).astype(jnp.int32)


def zero_of(values):
    return values[(0,) * values.ndim] * 0


def gather_near(shards):
    joined = jnp.concatenate(shards, axis=1)
    near = [joined] + [send(joined, along_first(r)) for r in (1, 2, 3)]
    wide = shards[0].shape[1]
    return jnp.stack([block[:, :wide] for block in near]), jnp.stack([block[:, wide:] for block in near])


def gather_far(near):
    halves = near[:2], near[2:]
    first = [send(half, along_second(r)) for half, r in zip(halves, (1, 3))]
    second = [
        send(jnp.stack([half, got]), along_second(r)) for half, got, r in zip(halves, first, (3, 1))
    ]
    return first, second


def gather_pieces(near, first, second, after):
    own = [near, first[0], first[1], second[0].reshape(4, *near.shape[1:]), second[1].reshape(4, *near.shape[1:])]
    return own + [send(piece + after, other_core()) for piece in own]


def gather_direct(near):
    return [near] + [send(near, along_second(r)) for r in (1, 2, 3)]


def with_other(own, after):
    return own + [send(piece + after if i else piece, other_core()) for i, piece in enumerate(own)]


DIRECT = tuple(tuple((r, j) for j in range(4)) for r in range(4))
PIECES = (
    ((0, 0), (0, 1), (0, 2), (0, 3)),
    ((1, 0), (1, 1)),
    ((3, 2), (3, 3)),
    ((3, 0), (3, 1), (2, 0), (2, 1)),
    ((1, 2), (1, 3), (2, 2), (2, 3)),
)
NP = 2 * len(PIECES)
ND = 2 * len(DIRECT)


def total_of(parts):
    summed = parts[0].astype(F32)
    for part in parts[1:]:
        summed = summed + part.astype(F32)
    return summed


def chip_sum(mine, other):
    other = send(other, other_core())
    return [total_of([mine[4 * j : 4 * j + 4], other[4 * j : 4 * j + 4]]).astype(BF16) for j in range(4)]


def scatter_first(groups):
    return [groups[0]] + [send(groups[r], along_first(r)) for r in (1, 2, 3)]


def scatter_rest(near, follow):
    close = total_of([near[0]] + [send(near[r], along_second(r)) for r in (1, 2, 3)]) + follow
    close = close.astype(BF16)
    wide = close.shape[1] // 2
    halves = []
    for half, order in ((close[:, :wide], (1, 3)), (close[:, wide:], (3, 1))):
        half = total_of([half, send(half, along_x(order[0]))]).astype(BF16)
        halves.append(total_of([half, send(half, along_x(order[1]))]))
    return jnp.concatenate(halves, axis=1)


def half_of_chip(values, c):
    return jnp.where(c == 0, values[0], values[1]) + send(jnp.where(c == 0, values[1], values[0]), other_core())


def finish_small(values, rows, c):
    values = total_of([values] + [send(values, along_first(r)) for r in (1, 2, 3)])
    other = send(values, other_core())
    mine, late = values[:rows], values[rows:] + other[rows:]
    other = other[:rows]
    return jnp.concatenate([jnp.where(c == 0, mine, other), jnp.where(c == 0, other, mine)]), late


def body(
    tables, log_mel, bucket_list, utterance_frames, stem_weight, first_gain, gate_proj, conv_kernel, second_gain,
    out_proj, cotangent,
):
    y, z, c = lax.axis_index("y"), lax.axis_index("z"), lax.axis_index("c")
    offsets = gather_offsets(y, z, c)
    slots = scatter_slots(y, z, c)
    tables = {name: jnp.asarray(value) for name, value in tables.items()}
    first_gain, second_gain = first_gain[None], second_gain[None]

    gate_near, out_near = gather_near((gate_proj, out_proj))
    outgoing = jnp.take(log_mel, bucket_list[0], axis=0) + zero_of(gate_near)
    arrived = lax.all_to_all(outgoing, ALL, split_axis=0, concat_axis=0, tiled=True)
    gate_far = gather_far(gate_near)
    stem_total, embedded, normed, normed_t, frames_t, spectrum, mix_grad = stem(
        gate_far[0][0], arrived.reshape(TOK * PATCH, MEL), utterance_frames, stem_weight, first_gain, conv_kernel, cotangent, tables
    )
    gate_pieces = gather_pieces(gate_near, *gate_far, zero_of(normed))
    out_near = out_near + sum(zero_of(piece) for piece in gate_far[1])
    out_own = gather_direct(out_near)
    value, gate, filtered = gate_forward(offsets, utterance_frames, gate_pieces, normed, spectrum, tables)
    out_pieces = with_other(out_own, zero_of(filtered).astype(BF16))
    out_mine, out_other, swished = out_grad(slots, out_own[1:], filtered, mix_grad, second_gain)
    filter_grad, second_grad = middle(offsets, out_pieces, filtered, mix_grad, second_gain)
    out_sums = chip_sum(out_mine, out_other)
    out_groups = scatter_first(out_sums)
    grads, nears, convs = [], [], []
    for begin, count in ((0, 4), (4, 2)):
        value_grad, gate_grad, mine, other, conv_grad = conv_back(
            slots, utterance_frames, out_sums[1:], value, gate, filter_grad, normed_t, spectrum, tables, begin, count
        )
        grads.append((value_grad, gate_grad))
        if begin:
            other = other + sum(zero_of(group) for group in out_groups[1:])
        nears.append((mine, send(other, other_core())))
        convs.append(conv_grad[:TAPS])
    gate_groups = chip_sums(nears)
    first_grad, stem_grad = stem_back(
        offsets, utterance_frames, gate_pieces, [pair[k] for k in range(2) for pair in grads], gate_groups[1:], embedded,
        stem_total, mix_grad, first_gain, frames_t,
    )
    early = jnp.concatenate([jnp.concatenate(convs, axis=1), second_grad], axis=0)
    early = half_of_chip(early.reshape(2, 16, D), c)
    follow = zero_of(first_grad)
    terms = [scatter_first(gate_groups), out_groups]
    near = jnp.concatenate([(total_of(term) + follow).astype(BF16) for term in terms], axis=-1)
    late = jnp.concatenate([first_grad, jnp.pad(stem_grad.reshape(1, -1), ((0, 0), (0, D - 16 * CH)))], axis=0)
    small = jnp.concatenate([early, late, jnp.zeros((6, D), F32)], axis=0)
    small = jnp.concatenate([small[:8], small[8:16], small[16:]], axis=1).astype(BF16)
    near = jnp.concatenate([near, jnp.broadcast_to(small[None], (4, *small.shape))], axis=1)
    output = mixed_out(offsets, utterance_frames, out_pieces, near, swished, embedded)
    sums = scatter_rest(near, zero_of(output).astype(F32))
    small = sums[ROWS:]
    early, late = finish_small(
        jnp.concatenate([small[:, :D], small[:, D : 2 * D], small[:2, 2 * D :]]), 16, c
    )
    sums = sums[:ROWS]
    blocks = [sums[:, i * CB : (i + 1) * CB] for i in range(2 * NB)]
    gate_sums = jnp.concatenate(blocks[::2] + blocks[1::2], axis=1)
    return (
        output, gate_sums, sums[:, 2 * D :], late[1, : 16 * CH].reshape(16, CH), late[0],
        early[:TAPS], early[TAPS],
    )


def solution(mesh):
    grid = Mesh(mesh.devices.reshape(4, 4, 4, 2), ALL)
    rows = ("y", "z", "c")
    return jax.shard_map(
        functools.partial(body, transforms()),
        mesh=grid,
        in_specs=(
            P(ALL, None, None), P(ALL, None), P(ALL), P(), P(), P(rows, None), P(), P(), P(rows, None), P(ALL, None),
        ),
        out_specs=(P(ALL, None), P(rows, None), P(rows, None), P(), P(), P(), P()),
        check_vma=False,
    )
```

```python
import functools

import jax
import jax.numpy as jnp
import numpy as np
from jax import lax
from jax.experimental import pallas as pl
from jax.experimental.pallas import tpu as pltpu
from jax.sharding import Mesh
from jax.sharding import PartitionSpec as P

PATCH = 4
UTT = 128
TOK = 512
NU = TOK // UTT
D = 1536
MEL = 128
CH = 48
TAPS = 31
HALF = TAPS // 2
EPS = 1e-05
ROWS = 48
CB = 256
NB = D // CB
ALL = ("x", "y", "z", "c")
F32 = jnp.float32
BF16 = jnp.bfloat16
MIB = 1024 * 1024
COST = 1

CYC = 144
BINS = CYC // 2 + 1
IM = 80
SPEC = 160


def hi_lo(values):
    high = values.astype(np.float32).astype(jnp.bfloat16)
    low = (values - high.astype(np.float64)).astype(np.float32).astype(jnp.bfloat16)
    return high, low


def side_by_side(values, three=False):
    high, low = hi_lo(values)
    parts = [high, low] + ([high] if three else [])
    return np.concatenate(parts, axis=1)


def transforms():
    angle = 2 * np.pi / CYC
    bins = np.arange(BINS)[:, None]
    places = np.arange(UTT)[None, :]
    offsets = np.arange(TAPS)[None, :] - HALF
    forward = np.zeros((SPEC, UTT))
    forward[:BINS] = np.cos(angle * bins * places)
    forward[IM : IM + BINS] = -np.sin(angle * bins * places)
    kernel = np.zeros((SPEC, 32))
    kernel[:BINS, :TAPS] = np.cos(angle * bins * offsets)
    kernel[IM : IM + BINS, :TAPS] = np.sin(angle * bins * offsets)
    weight = np.full((BINS, 1), 2.0 / CYC)
    weight[0] = weight[-1] = 1.0 / CYC
    back = np.zeros((UTT, SPEC))
    back[:, :BINS] = (weight * np.cos(angle * bins * places)).T
    back[:, IM : IM + BINS] = -(weight * np.sin(angle * bins * places)).T
    return {
        "fwd": side_by_side(forward),
        "inv": side_by_side(back),
        "fwd_t": side_by_side(forward.T),
        "inv_t": side_by_side(back.T),
        "ker": side_by_side(kernel, True),
        "ker_t": side_by_side(kernel.T, True),
    }


def twice(values):
    narrow = values.astype(BF16)
    return jnp.concatenate([narrow, narrow], axis=0)


def thrice(values):
    high = values.astype(BF16)
    low = (values - high.astype(F32)).astype(BF16)
    return jnp.concatenate([high, high, low], axis=0)


def mm(left, right):
    return jnp.dot(left, right, preferred_element_type=F32)


def mm_nt(left, right):
    return lax.dot_general(left, right, (((1,), (1,)), ((), ())), preferred_element_type=F32)


def keep(limit, shape):
    return lax.broadcasted_iota(jnp.int32, shape, 0) < limit


def row_mean(values):
    return jnp.sum(values, axis=-1, keepdims=True) * (1.0 / D)


def normalise(values):
    centred = values - row_mean(values)
    scale = lax.rsqrt(row_mean(centred * centred) + EPS)
    return centred * scale, scale


def normalise_back(grad, unit, scale):
    return scale * (grad - row_mean(grad) - unit * row_mean(grad * unit))


def stem_masks(rows, cols):
    row = lax.broadcasted_iota(jnp.int32, (rows, cols), 0)
    col = lax.broadcasted_iota(jnp.int32, (rows, cols), 1)
    group = (row % MEL) // PATCH
    first = group * CH
    return (col >= first) & (col < first + CH)


def tap_select(rows):
    row = lax.broadcasted_iota(jnp.int32, (rows, 16), 0)
    tap = lax.broadcasted_iota(jnp.int32, (rows, 16), 1)
    return (tap == PATCH * (row // MEL) + row % PATCH).astype(F32).astype(BF16)


def channel_select():
    row = lax.broadcasted_iota(jnp.int32, (CH, D), 0)
    col = lax.broadcasted_iota(jnp.int32, (CH, D), 1)
    return (col % CH == row).astype(F32).astype(BF16)


def stem_kernel(
    unused, frames_of, arrived, stem_weight, first_gain, conv_kernel, cotangent, ker,
    stem_total, embedded, normed, normed_t, frames_t, spectrum, mix_grad, wide, big,
):
    wide[...] = arrived[...].astype(F32)
    taps = mm(tap_select(TOK), stem_weight[...]).astype(BF16)
    spread = mm(taps, channel_select())
    big[...] = jnp.where(stem_masks(TOK, D), spread, 0.0).astype(BF16)
    padded = jnp.concatenate([conv_kernel[...], jnp.zeros((1, D), F32)], axis=0)
    spectrum[...] = mm(ker[...], thrice(padded))

    def one(u, carry):
        base = pl.multiple_of(u * UTT, UTT)
        rows = pl.ds(base, UTT)
        parts = [wide[pl.ds(base * PATCH + i, UTT, stride=PATCH), :].astype(BF16) for i in range(PATCH)]
        frames = jnp.concatenate(parts, axis=1)
        total = mm(frames, big[...])
        stem_total[rows, :] = total
        valid = keep(frames_of[u] // PATCH, (UTT, D))
        kept = jnp.where(valid, total * jax.nn.sigmoid(total), 0.0).astype(BF16)
        embedded[rows, :] = kept
        unit, scale = normalise(kept.astype(F32))
        narrow = (unit * first_gain[...]).astype(BF16)
        normed[rows, :] = narrow
        normed_t[:, rows] = narrow.T
        frames_t[:, rows] = frames.T
        mix_grad[rows, :] = jnp.where(valid, cotangent[rows, :].astype(F32), 0.0).astype(BF16)
        return carry

    lax.fori_loop(0, NU, one, 0)


def assembly(offsets, pieces, held, sems):
    copies = []
    layout = PIECES if len(pieces) == NP else DIRECT
    for p, piece in enumerate(pieces):
        for j, (second, first) in enumerate(layout[p % len(layout)]):
            block = p // len(layout) * 16 + second * 4 + first
            start = pl.multiple_of(offsets[block], 16)
            copies.append(pltpu.make_async_copy(piece.at[j], held.at[pl.ds(start, ROWS), :], sems.at[block]))
    return copies


def assemble(offsets, pieces, held, sems):
    copies = assembly(offsets, pieces, held, sems)
    for copy in copies:
        copy.start()
    for copy in copies:
        copy.wait()


def gate_kernel(offsets, frames_of, *refs):
    pieces, refs = refs[:NP], refs[NP:]
    normed, spectrum, fwd, inv, value, gate, filtered, held, sems = refs
    n = pl.program_id(0)

    @pl.when(n == 0)
    def _():
        assemble(offsets, pieces, held, sems)

    start = pl.multiple_of(n * CB, CB)
    value[...] = mm(normed[...], held[:, pl.ds(start, CB)])
    gate[...] = mm(normed[...], held[:, pl.ds(pl.multiple_of(D + start, CB), CB)])
    re, im = spectrum[:IM, :], spectrum[IM:, :]
    for u in range(NU):
        rows = slice(u * UTT, (u + 1) * UTT)
        gated = value[rows, :] * jax.nn.sigmoid(gate[rows, :])
        gated = jnp.where(keep(frames_of[u] // PATCH, (UTT, CB)), gated, 0.0)
        seen = mm(fwd[...], twice(gated))
        a, b = seen[:IM], seen[IM:]
        moved = jnp.concatenate([a * re - b * im, a * im + b * re], axis=0)
        filtered[rows, :] = mm(inv[...], twice(moved))


def block_start(slots, i, flip):
    core = slots[32] if flip == 0 else 1 - slots[32]
    return pl.multiple_of((2 * i + core) * ROWS, 16)


def out_kernel(slots, unused_1, unused_2, unused_3, filtered, mix_grad, second_gain, mine, other, swished, turned, term):
    def ahead(u, carry):
        rows = pl.ds(pl.multiple_of(u * UTT, UTT), UTT)
        unit, unused = normalise(filtered[rows, :])
        z = unit * second_gain[...]
        narrow = (z * jax.nn.sigmoid(z)).astype(BF16)
        swished[rows, :] = narrow
        turned[:, rows] = narrow.T
        return carry

    lax.fori_loop(0, NU, ahead, 0)

    def product(n, carry):
        cols = pl.ds(pl.multiple_of(n * CB, CB), CB)
        term[...] = mm(turned[...], mix_grad[:, cols]).astype(BF16)
        for i in range(16):
            mine[slots[i], :, cols] = term[pl.ds(block_start(slots, i, 0), ROWS), :]
            other[slots[16 + i], :, cols] = term[pl.ds(block_start(slots, i, 1), ROWS), :]
        return carry

    lax.fori_loop(0, NB, product, 0)


def mid_kernel(offsets, *refs):
    pieces, refs = refs[:ND], refs[ND:]
    filtered, mix_grad, second_gain, filter_grad, second_grad, held, sems, back, slope, scales = refs
    copies = assembly(offsets, pieces, held, sems)
    for copy in copies:
        copy.start()
    second_grad[...] = jnp.zeros((1, D), F32)

    def ahead(u, carry):
        rows = pl.ds(pl.multiple_of(u * UTT, UTT), UTT)
        unit, scale = normalise(filtered[rows, :])
        z = unit * second_gain[...]
        sig = jax.nn.sigmoid(z)
        slope[rows, :] = sig * (1.0 + z * (1.0 - sig))
        filter_grad[rows, :] = unit
        scales[rows, :] = jnp.broadcast_to(scale, (UTT, 128))
        return carry

    lax.fori_loop(0, NU, ahead, 0)
    for copy in copies:
        copy.wait()

    def product(n, carry):
        cols = pl.ds(pl.multiple_of(n * 2 * CB, 2 * CB), 2 * CB)
        back[:, cols] = mm_nt(mix_grad[...], held[cols, :])
        return carry

    lax.fori_loop(0, NB // 2, product, 0)

    def behind(u, carry):
        rows = pl.ds(pl.multiple_of(u * UTT, UTT), UTT)
        unit = filter_grad[rows, :]
        dz = back[rows, :] * slope[rows, :]
        second_grad[...] += jnp.sum(dz * unit, axis=0, keepdims=True)
        filter_grad[rows, :] = normalise_back(dz * second_gain[...], unit, scales[rows, :1])
        return carry

    lax.fori_loop(0, NU, behind, 0)


def conv_back_kernel(
    slots, frames_of, unused_1, unused_2, unused_3, value, gate, filter_grad, normed_t, spectrum, fwd, inv_t, fwd_t, ker_t,
    value_grad, gate_grad, mine, other, conv_grad, term,
):
    re, im = spectrum[:IM, :], spectrum[IM:, :]
    sum_re = jnp.zeros((IM, CB), F32)
    sum_im = jnp.zeros((IM, CB), F32)
    for u in range(NU):
        rows = slice(u * UTT, (u + 1) * UTT)
        valid = keep(frames_of[u] // PATCH, (UTT, CB))
        v = value[rows, :]
        sig = jax.nn.sigmoid(gate[rows, :])
        gated = jnp.where(valid, v * sig, 0.0)
        seen = mm(fwd[...], twice(gated))
        a, b = seen[:IM], seen[IM:]
        grad = mm(inv_t[...], twice(filter_grad[rows, :]))
        da, db = grad[:IM], grad[IM:]
        sum_re = sum_re + a * da + b * db
        sum_im = sum_im + a * db - b * da
        spread = jnp.concatenate([re * da + im * db, re * db - im * da], axis=0)
        gated_grad = jnp.where(valid, mm(fwd_t[...], twice(spread)), 0.0)
        part = gated_grad * sig
        value_grad[rows, :] = part.astype(BF16)
        gate_grad[rows, :] = (part * v * (1.0 - sig)).astype(BF16)
    conv_grad[...] = mm(ker_t[...], thrice(jnp.concatenate([sum_re, sum_im], axis=0)))
    for h, grad_ref in enumerate((value_grad, gate_grad)):
        term[...] = mm(normed_t[...], grad_ref[...]).astype(BF16)
        for i in range(16):
            cols = slice(h * CB, (h + 1) * CB)
            mine[slots[i], :, cols] = term[pl.ds(block_start(slots, i, 0), ROWS), :]
            other[slots[16 + i], :, cols] = term[pl.ds(block_start(slots, i, 1), ROWS), :]


def stem_back_kernel(offsets, frames_of, *refs):
    pieces, refs = refs[:NP], refs[NP:]
    grads, refs = refs[:4], refs[4:]
    (unused_1, unused_2, unused_3, embedded, stem_total, mix_grad, first_gain, frames_t,
     first_grad, stem_grad, held, sems, back, pre_grad) = refs
    assemble(offsets, pieces, held, sems)
    first_grad[...] = jnp.zeros((1, D), F32)

    def product(n, carry):
        cols = pl.ds(pl.multiple_of(n * CB, CB), CB)
        total = jnp.zeros((TOK, CB), F32)
        begin = 0
        for grad in grads:
            total = total + mm_nt(grad[...], held[cols, begin : begin + grad.shape[1]])
            begin += grad.shape[1]
        back[:, cols] = total
        return carry

    lax.fori_loop(0, NB, product, 0)

    def behind(u, carry):
        rows = pl.ds(pl.multiple_of(u * UTT, UTT), UTT)
        unit, scale = normalise(embedded[rows, :].astype(F32))
        grad = back[rows, :]
        first_grad[...] += jnp.sum(grad * unit, axis=0, keepdims=True)
        grad = normalise_back(grad * first_gain[...], unit, scale) + mix_grad[rows, :].astype(F32)
        total = stem_total[rows, :]
        sig = jax.nn.sigmoid(total)
        grad = grad * (sig * (1.0 + total * (1.0 - sig)))
        valid = keep(frames_of[u] // PATCH, (UTT, D))
        pre_grad[rows, :] = jnp.where(valid, grad, 0.0).astype(BF16)
        return carry

    lax.fori_loop(0, NU, behind, 0)
    outer = mm(frames_t[...], pre_grad[...])
    outer = jnp.where(stem_masks(TOK, D), outer, 0.0)
    pick = tap_select(TOK).T
    folded = mm(jnp.concatenate([pick, pick], axis=1), split_rows(outer))
    channel = channel_select()
    high = folded.astype(BF16)
    low = (folded - high.astype(F32)).astype(BF16)
    stem_grad[...] = mm_nt(high, channel) + mm_nt(low, channel)


def split_rows(values):
    high = values.astype(BF16)
    low = (values - high.astype(F32)).astype(BF16)
    return jnp.concatenate([high, low], axis=0)


def mixed_kernel(offsets, frames_of, *refs):
    pieces, refs = refs[:ND], refs[ND:]
    unused, swished, embedded, output, held, sems = refs
    assemble(offsets, pieces, held, sems)

    def product(n, carry):
        cols = pl.ds(pl.multiple_of(n * CB, CB), CB)
        mixed = mm(swished[...], held[:, cols])
        for u in range(NU):
            rows = slice(u * UTT, (u + 1) * UTT)
            total = embedded[rows, cols].astype(F32) + mixed[rows]
            valid = keep(frames_of[u] // PATCH, (UTT, CB))
            output[rows, cols] = jnp.where(valid, total, 0.0).astype(BF16)
        return carry

    lax.fori_loop(0, NB, product, 0)


def chip_sum_kernel(mine_1, other_1, mine_2, other_2, *groups):
    wide = mine_1.shape[-1]
    for r, group in enumerate(groups):
        group[0, :, :wide] = (mine_1[r, 0].astype(F32) + other_1[r, 0].astype(F32)).astype(BF16)
        group[0, :, wide:] = (mine_2[r, 0].astype(F32) + other_2[r, 0].astype(F32)).astype(BF16)


SMEM = pl.BlockSpec(memory_space=pltpu.SMEM)
ANY = pl.BlockSpec(memory_space=pl.ANY)
VMEM = pl.BlockSpec(memory_space=pltpu.VMEM)


def shaped(shape, dtype):
    return jax.ShapeDtypeStruct(shape, dtype)


def call(kernel, name, operands, in_specs, outs, out_specs, scratch, flops, nbytes, vmem, grid=None):
    more = {} if grid is None else {"grid": grid}
    return pl.pallas_call(
        kernel,
        name=name,
        out_shape=outs,
        in_specs=in_specs,
        out_specs=out_specs,
        scratch_shapes=scratch,
        compiler_params=pltpu.CompilerParams(vmem_limit_bytes=vmem * MIB),
        cost_estimate=pl.CostEstimate(flops=flops // COST, bytes_accessed=nbytes // COST, transcendentals=0),
        **more,
    )(*operands)


def stem(before, arrived, frames_of, stem_weight, first_gain, conv_kernel, cotangent, tables):
    outs = [
        shaped((TOK, D), F32), shaped((TOK, D), BF16), shaped((TOK, D), BF16), shaped((D, TOK), BF16),
        shaped((TOK, TOK), BF16), shaped((SPEC, D), F32), shaped((TOK, D), BF16),
    ]
    return call(
        stem_kernel, "stem",
        (before, frames_of, arrived, stem_weight, first_gain, conv_kernel, cotangent, tables["ker"]),
        [ANY, SMEM] + [VMEM] * 6, outs, [VMEM] * 7,
        [pltpu.VMEM((TOK * PATCH, MEL), F32), pltpu.VMEM((TOK, D), BF16)],
        2 * TOK * TOK * D, 14 * MIB, 26,
    )


def gate_forward(offsets, frames_of, pieces, normed, spectrum, tables):
    whole = lambda n: (0, 0)
    block = lambda n: (0, n)
    return call(
        gate_kernel, "gate",
        (offsets, frames_of, *pieces, normed, spectrum, tables["fwd"], tables["inv"]),
        [SMEM, SMEM] + [ANY] * NP
        + [pl.BlockSpec((TOK, D), whole), pl.BlockSpec((SPEC, CB), block),
           pl.BlockSpec(tables["fwd"].shape, whole), pl.BlockSpec(tables["inv"].shape, whole)],
        [shaped((TOK, D), F32)] * 3, [pl.BlockSpec((TOK, CB), block)] * 3,
        [pltpu.VMEM((D, 2 * D), BF16), pltpu.SemaphoreType.DMA((32,))],
        2 * TOK * D * 2 * D, 22 * MIB, 26, grid=(NB,),
    )


def out_grad(slots, before, filtered, mix_grad, second_gain):
    half = shaped((16, ROWS, D), BF16)
    return call(
        out_kernel, "out_grad", (slots, *before, filtered, mix_grad, second_gain),
        [SMEM] + [ANY] * 3 + [VMEM] * 3, [half, half, shaped((TOK, D), BF16)], [VMEM] * 3,
        [pltpu.VMEM((D, TOK), BF16), pltpu.VMEM((D, CB), BF16)],
        16 * 2 * TOK * D * D, 16 * 11 * MIB, 24,
    )


def middle(offsets, pieces, filtered, mix_grad, second_gain):
    return call(
        mid_kernel, "middle", (offsets, *pieces, filtered, mix_grad, second_gain),
        [SMEM] + [ANY] * ND + [VMEM] * 3, [shaped((TOK, D), F32), shaped((1, D), F32)], [VMEM] * 2,
        [pltpu.VMEM((D, D), BF16), pltpu.SemaphoreType.DMA((32,)), pltpu.VMEM((TOK, D), F32),
         pltpu.VMEM((TOK, D), F32), pltpu.VMEM((TOK, 128), F32)],
        16 * 2 * TOK * D * D, 16 * 13 * MIB, 28,
    )


def conv_back(slots, frames_of, before, value, gate, filter_grad, normed_t, spectrum, tables, begin, count):
    whole = lambda n: (0, 0)
    block = lambda n: (0, n + begin)
    own = lambda n: (0, n)
    width = count * CB
    names = ("fwd", "inv_t", "fwd_t", "ker_t")
    half = shaped((16, ROWS, 2 * width), BF16)
    half_spec = pl.BlockSpec((16, ROWS, 2 * CB), lambda n: (0, 0, n))
    outs = [shaped((TOK, width), BF16), shaped((TOK, width), BF16), half, half, shaped((32, width), F32)]
    return call(
        conv_back_kernel, "conv_back",
        (slots, frames_of, *before, value, gate, filter_grad, normed_t, spectrum, *[tables[k] for k in names]),
        [SMEM, SMEM, ANY, ANY, ANY] + [pl.BlockSpec((TOK, CB), block)] * 3
        + [pl.BlockSpec((D, TOK), whole), pl.BlockSpec((SPEC, CB), block)]
        + [pl.BlockSpec(tables[k].shape, whole) for k in names],
        outs,
        [pl.BlockSpec((TOK, CB), own)] * 2 + [half_spec, half_spec, pl.BlockSpec((32, CB), own)],
        [pltpu.VMEM((D, CB), BF16)], 2 * TOK * D * width * 2 * 16, 22 * MIB * count // NB * 16, 22, grid=(count,),
    )


def stem_back(offsets, frames_of, pieces, grads, before, embedded, stem_total, mix_grad, first_gain, frames_t):
    return call(
        stem_back_kernel, "stem_back",
        (offsets, frames_of, *pieces, *grads, *before, embedded, stem_total, mix_grad, first_gain, frames_t),
        [SMEM, SMEM] + [ANY] * NP + [VMEM] * 4 + [ANY] * 3 + [VMEM] * 5,
        [shaped((1, D), F32), shaped((16, CH), F32)], [VMEM] * 2,
        [pltpu.VMEM((D, 2 * D), BF16), pltpu.SemaphoreType.DMA((32,)), pltpu.VMEM((TOK, D), F32), pltpu.VMEM((TOK, D), BF16)],
        16 * 2 * TOK * D * 2 * D, 16 * 20 * MIB, 36,
    )


def mixed_out(offsets, frames_of, pieces, before, swished, embedded):
    return call(
        mixed_kernel, "mixed",
        (offsets, frames_of, *pieces, before, swished, embedded),
        [SMEM, SMEM] + [ANY] * (ND + 1) + [VMEM] * 2,
        shaped((TOK, D), BF16), VMEM,
        [pltpu.VMEM((D, D), BF16), pltpu.SemaphoreType.DMA((32,))],
        2 * TOK * D * D, 10 * MIB, 18,
    )


def chip_sums(parts):
    operands = [value.reshape(4, 4, *value.shape[1:]) for part in parts for value in part]
    width = 2 * D
    spec = lambda value: pl.BlockSpec((4, 1, *value.shape[2:]), lambda m: (0, m, 0, 0))
    return call(
        chip_sum_kernel, "chip_sum", operands, [spec(value) for value in operands],
        [shaped((4, ROWS, width), BF16)] * 4, [pl.BlockSpec((1, ROWS, width), lambda m: (m, 0, 0))] * 4,
        [], 16 * ROWS * width, 14 * MIB, 18, grid=(4,),
    )


def place(x, y, z, c):
    return ((x % 4 * 4 + y % 4) * 4 + z % 4) * 2 + c


def pairs(step):
    found = []
    for x in range(4):
        for y in range(4):
            for z in range(4):
                for c in range(2):
                    found.append((place(x, y, z, c), step(x, y, z, c)))
    return found


def along_first(r):
    return pairs(lambda x, y, z, c: place(x, y ^ (r * c), z ^ (r * (1 - c)), c))


def along_second(r):
    return pairs(lambda x, y, z, c: place(x, y ^ (r * (1 - c)), z ^ (r * c), c))


def along_x(r):
    return pairs(lambda x, y, z, c: place(x ^ r, y, z, c))


def other_core():
    return pairs(lambda x, y, z, c: place(x, y, z, 1 - c))


def send(values, where):
    return lax.ppermute(values, ALL, where)


def gather_offsets(y, z, c):
    m, j = np.divmod(np.arange(16, dtype=np.int32), 4)

    def of(core):
        row_y = y ^ jnp.where(core == 0, m, j)
        row_z = z ^ jnp.where(core == 0, j, m)
        return ((row_y * 4 + row_z) * 2 + core) * ROWS

    return jnp.concatenate([of(c), of(1 - c)]).astype(jnp.int32)


def scatter_slots(y, z, c):
    block = np.arange(16, dtype=np.int32)
    far_y, far_z = (block // 4) ^ y, (block % 4) ^ z

    def of(core):
        return jnp.where(core == 0, far_z * 4 + far_y, far_y * 4 + far_z)

    return jnp.concatenate([of(c), of(1 - c), c[None]]).astype(jnp.int32)


def zero_of(values):
    return values[(0,) * values.ndim] * 0


def gather_near(shard):
    return jnp.stack([shard] + [send(shard, along_first(r)) for r in (1, 2, 3)])


def gather_far(near):
    halves = near[:2], near[2:]
    first = [send(half, along_second(r)) for half, r in zip(halves, (1, 3))]
    second = [
        send(jnp.stack([half, got]), along_second(r)) for half, got, r in zip(halves, first, (3, 1))
    ]
    return first, second


def gather_pieces(near, first, second, after):
    own = [near, first[0], first[1], second[0].reshape(4, *near.shape[1:]), second[1].reshape(4, *near.shape[1:])]
    return own + [send(piece + after, other_core()) for piece in own]


def gather_direct(near):
    return [near] + [send(near, along_second(r)) for r in (1, 2, 3)]


def with_other(own, after):
    return own + [send(piece + after if i else piece, other_core()) for i, piece in enumerate(own)]


DIRECT = tuple(tuple((r, j) for j in range(4)) for r in range(4))
PIECES = (
    ((0, 0), (0, 1), (0, 2), (0, 3)),
    ((1, 0), (1, 1)),
    ((3, 2), (3, 3)),
    ((3, 0), (3, 1), (2, 0), (2, 1)),
    ((1, 2), (1, 3), (2, 2), (2, 3)),
)
NP = 2 * len(PIECES)
ND = 2 * len(DIRECT)


def total_of(parts):
    summed = parts[0].astype(F32)
    for part in parts[1:]:
        summed = summed + part.astype(F32)
    return summed


def chip_sum(mine, other):
    other = send(other, other_core())
    return [total_of([mine[4 * j : 4 * j + 4], other[4 * j : 4 * j + 4]]).astype(BF16) for j in range(4)]


def scatter_first(groups):
    return [groups[0]] + [send(groups[r], along_first(r)) for r in (1, 2, 3)]


def scatter_rest(near, follow):
    close = total_of([near[0]] + [send(near[r], along_second(r)) for r in (1, 2, 3)]) + follow
    close = close.astype(BF16)
    wide = close.shape[1] // 2
    halves = []
    for half, order in ((close[:, :wide], (1, 3)), (close[:, wide:], (3, 1))):
        half = total_of([half, send(half, along_x(order[0]))]).astype(BF16)
        halves.append(total_of([half, send(half, along_x(order[1]))]))
    return jnp.concatenate(halves, axis=1)


def half_of_chip(values, c):
    return jnp.where(c == 0, values[0], values[1]) + send(jnp.where(c == 0, values[1], values[0]), other_core())


def finish_small(values, rows, c):
    values = total_of([values] + [send(values, along_first(r)) for r in (1, 2, 3)])
    other = send(values, other_core())
    mine, late = values[:rows], values[rows:] + other[rows:]
    other = other[:rows]
    return jnp.concatenate([jnp.where(c == 0, mine, other), jnp.where(c == 0, other, mine)]), late


def body(
    tables, log_mel, bucket_list, utterance_frames, stem_weight, first_gain, gate_proj, conv_kernel, second_gain,
    out_proj, cotangent,
):
    y, z, c = lax.axis_index("y"), lax.axis_index("z"), lax.axis_index("c")
    offsets = gather_offsets(y, z, c)
    slots = scatter_slots(y, z, c)
    tables = {name: jnp.asarray(value) for name, value in tables.items()}
    first_gain, second_gain = first_gain[None], second_gain[None]

    gate_near = gather_near(gate_proj)
    outgoing = jnp.take(log_mel, bucket_list[0], axis=0) + zero_of(gate_near[1])
    arrived = lax.all_to_all(outgoing, ALL, split_axis=0, concat_axis=0, tiled=True)
    gate_far = gather_far(gate_near)
    stem_total, embedded, normed, normed_t, frames_t, spectrum, mix_grad = stem(
        gate_far[0][0], arrived.reshape(TOK * PATCH, MEL), utterance_frames, stem_weight, first_gain, conv_kernel, cotangent, tables
    )
    gate_pieces = gather_pieces(gate_near, *gate_far, zero_of(normed))
    out_near = gather_near(out_proj + zero_of(gate_far[0][0])) + sum(zero_of(piece) for piece in gate_far[1])
    out_own = gather_direct(out_near)
    value, gate, filtered = gate_forward(offsets, utterance_frames, gate_pieces, normed, spectrum, tables)
    out_pieces = with_other(out_own, zero_of(filtered).astype(BF16))
    out_mine, out_other, swished = out_grad(slots, out_own[1:], filtered, mix_grad, second_gain)
    filter_grad, second_grad = middle(offsets, out_pieces, filtered, mix_grad, second_gain)
    out_sums = chip_sum(out_mine, out_other)
    out_groups = scatter_first(out_sums)
    grads, nears, convs = [], [], []
    for begin, count in ((0, 4), (4, 2)):
        value_grad, gate_grad, mine, other, conv_grad = conv_back(
            slots, utterance_frames, out_sums[1:], value, gate, filter_grad, normed_t, spectrum, tables, begin, count
        )
        grads.append((value_grad, gate_grad))
        if begin:
            other = other + sum(zero_of(group) for group in out_groups[1:])
        nears.append((mine, send(other, other_core())))
        convs.append(conv_grad[:TAPS])
    gate_groups = chip_sums(nears)
    first_grad, stem_grad = stem_back(
        offsets, utterance_frames, gate_pieces, [pair[k] for k in range(2) for pair in grads], gate_groups[1:], embedded,
        stem_total, mix_grad, first_gain, frames_t,
    )
    early = jnp.concatenate([jnp.concatenate(convs, axis=1), second_grad], axis=0)
    early = half_of_chip(early.reshape(2, 16, D), c)
    follow = zero_of(first_grad)
    terms = [scatter_first(gate_groups), out_groups]
    near = jnp.concatenate([(total_of(term) + follow).astype(BF16) for term in terms], axis=-1)
    late = jnp.concatenate([first_grad, jnp.pad(stem_grad.reshape(1, -1), ((0, 0), (0, D - 16 * CH)))], axis=0)
    small = jnp.concatenate([early, late, jnp.zeros((6, D), F32)], axis=0)
    small = jnp.concatenate([small[:8], small[8:16], small[16:]], axis=1).astype(BF16)
    near = jnp.concatenate([near, jnp.broadcast_to(small[None], (4, *small.shape))], axis=1)
    output = mixed_out(offsets, utterance_frames, out_pieces, near, swished, embedded)
    sums = scatter_rest(near, zero_of(output).astype(F32))
    small = sums[ROWS:]
    early, late = finish_small(
        jnp.concatenate([small[:, :D], small[:, D : 2 * D], small[:2, 2 * D :]]), 16, c
    )
    sums = sums[:ROWS]
    blocks = [sums[:, i * CB : (i + 1) * CB] for i in range(2 * NB)]
    gate_sums = jnp.concatenate(blocks[::2] + blocks[1::2], axis=1)
    return (
        output, gate_sums, sums[:, 2 * D :], late[1, : 16 * CH].reshape(16, CH), late[0],
        early[:TAPS], early[TAPS],
    )


def solution(mesh):
    grid = Mesh(mesh.devices.reshape(4, 4, 4, 2), ALL)
    rows = ("y", "z", "c")
    return jax.shard_map(
        functools.partial(body, transforms()),
        mesh=grid,
        in_specs=(
            P(ALL, None, None), P(ALL, None), P(ALL), P(), P(), P(rows, None), P(), P(), P(rows, None), P(ALL, None),
        ),
        out_specs=(P(ALL, None), P(rows, None), P(rows, None), P(), P(), P(), P()),
        check_vma=False,
    )
```

```python
import functools

import jax
import jax.numpy as jnp
import numpy as np
from jax import lax
from jax.experimental import pallas as pl
from jax.experimental.pallas import tpu as pltpu
from jax.sharding import Mesh
from jax.sharding import PartitionSpec as P

PATCH = 4
UTT = 128
TOK = 512
NU = TOK // UTT
D = 1536
MEL = 128
CH = 48
TAPS = 31
HALF = TAPS // 2
EPS = 1e-05
ROWS = 48
CB = 256
NB = D // CB
ALL = ("x", "y", "z", "c")
F32 = jnp.float32
BF16 = jnp.bfloat16
MIB = 1024 * 1024
COST = 1

CYC = 144
BINS = CYC // 2 + 1
IM = 80
SPEC = 160


def hi_lo(values):
    high = values.astype(np.float32).astype(jnp.bfloat16)
    low = (values - high.astype(np.float64)).astype(np.float32).astype(jnp.bfloat16)
    return high, low


def side_by_side(values, three=False):
    high, low = hi_lo(values)
    parts = [high, low] + ([high] if three else [])
    return np.concatenate(parts, axis=1)


def transforms():
    angle = 2 * np.pi / CYC
    bins = np.arange(BINS)[:, None]
    places = np.arange(UTT)[None, :]
    offsets = np.arange(TAPS)[None, :] - HALF
    forward = np.zeros((SPEC, UTT))
    forward[:BINS] = np.cos(angle * bins * places)
    forward[IM : IM + BINS] = -np.sin(angle * bins * places)
    kernel = np.zeros((SPEC, 32))
    kernel[:BINS, :TAPS] = np.cos(angle * bins * offsets)
    kernel[IM : IM + BINS, :TAPS] = np.sin(angle * bins * offsets)
    weight = np.full((BINS, 1), 2.0 / CYC)
    weight[0] = weight[-1] = 1.0 / CYC
    back = np.zeros((UTT, SPEC))
    back[:, :BINS] = (weight * np.cos(angle * bins * places)).T
    back[:, IM : IM + BINS] = -(weight * np.sin(angle * bins * places)).T
    return {
        "fwd": side_by_side(forward),
        "inv": side_by_side(back),
        "fwd_t": side_by_side(forward.T),
        "inv_t": side_by_side(back.T),
        "ker": side_by_side(kernel, True),
        "ker_t": side_by_side(kernel.T, True),
    }


def twice(values):
    narrow = values.astype(BF16)
    return jnp.concatenate([narrow, narrow], axis=0)


def thrice(values):
    high = values.astype(BF16)
    low = (values - high.astype(F32)).astype(BF16)
    return jnp.concatenate([high, high, low], axis=0)


def mm(left, right):
    return jnp.dot(left, right, preferred_element_type=F32)


def mm_nt(left, right):
    return lax.dot_general(left, right, (((1,), (1,)), ((), ())), preferred_element_type=F32)


def keep(limit, shape):
    return lax.broadcasted_iota(jnp.int32, shape, 0) < limit


def row_mean(values):
    return jnp.sum(values, axis=-1, keepdims=True) * (1.0 / D)


def normalise(values):
    centred = values - row_mean(values)
    scale = lax.rsqrt(row_mean(centred * centred) + EPS)
    return centred * scale, scale


def normalise_back(grad, unit, scale):
    return scale * (grad - row_mean(grad) - unit * row_mean(grad * unit))


def stem_masks(rows, cols):
    row = lax.broadcasted_iota(jnp.int32, (rows, cols), 0)
    col = lax.broadcasted_iota(jnp.int32, (rows, cols), 1)
    group = (row % MEL) // PATCH
    first = group * CH
    return (col >= first) & (col < first + CH)


def tap_select(rows):
    row = lax.broadcasted_iota(jnp.int32, (rows, 16), 0)
    tap = lax.broadcasted_iota(jnp.int32, (rows, 16), 1)
    return (tap == PATCH * (row // MEL) + row % PATCH).astype(F32).astype(BF16)


def channel_select():
    row = lax.broadcasted_iota(jnp.int32, (CH, D), 0)
    col = lax.broadcasted_iota(jnp.int32, (CH, D), 1)
    return (col % CH == row).astype(F32).astype(BF16)


def stem_kernel(
    unused, frames_of, arrived, stem_weight, first_gain, conv_kernel, cotangent, ker,
    stem_total, embedded, normed, normed_t, frames_t, spectrum, mix_grad, wide, big,
):
    wide[...] = arrived[...].astype(F32)
    taps = mm(tap_select(TOK), stem_weight[...]).astype(BF16)
    spread = mm(taps, channel_select())
    big[...] = jnp.where(stem_masks(TOK, D), spread, 0.0).astype(BF16)
    padded = jnp.concatenate([conv_kernel[...], jnp.zeros((1, D), F32)], axis=0)
    spectrum[...] = mm(ker[...], thrice(padded))

    def one(u, carry):
        base = pl.multiple_of(u * UTT, UTT)
        rows = pl.ds(base, UTT)
        parts = [wide[pl.ds(base * PATCH + i, UTT, stride=PATCH), :].astype(BF16) for i in range(PATCH)]
        frames = jnp.concatenate(parts, axis=1)
        total = mm(frames, big[...])
        stem_total[rows, :] = total
        valid = keep(frames_of[u] // PATCH, (UTT, D))
        kept = jnp.where(valid, total * jax.nn.sigmoid(total), 0.0).astype(BF16)
        embedded[rows, :] = kept
        unit, scale = normalise(kept.astype(F32))
        narrow = (unit * first_gain[...]).astype(BF16)
        normed[rows, :] = narrow
        normed_t[:, rows] = narrow.T
        frames_t[:, rows] = frames.T
        mix_grad[rows, :] = jnp.where(valid, cotangent[rows, :].astype(F32), 0.0).astype(BF16)
        return carry

    lax.fori_loop(0, NU, one, 0)


def assembly(offsets, pieces, held, sems):
    copies = []
    layout = PIECES if len(pieces) == NP else DIRECT
    for p, piece in enumerate(pieces):
        for j, (second, first) in enumerate(layout[p % len(layout)]):
            block = p // len(layout) * 16 + second * 4 + first
            start = pl.multiple_of(offsets[block], 16)
            copies.append(pltpu.make_async_copy(piece.at[j], held.at[pl.ds(start, ROWS), :], sems.at[block]))
    return copies


def assemble(offsets, pieces, held, sems):
    copies = assembly(offsets, pieces, held, sems)
    for copy in copies:
        copy.start()
    for copy in copies:
        copy.wait()


def gate_kernel(offsets, frames_of, *refs):
    pieces, refs = refs[:NP], refs[NP:]
    normed, spectrum, fwd, inv, value, gate, filtered, held, sems = refs
    n = pl.program_id(0)

    @pl.when(n == 0)
    def _():
        assemble(offsets, pieces, held, sems)

    start = pl.multiple_of(n * CB, CB)
    value[...] = mm(normed[...], held[:, pl.ds(start, CB)])
    gate[...] = mm(normed[...], held[:, pl.ds(pl.multiple_of(D + start, CB), CB)])
    re, im = spectrum[:IM, :], spectrum[IM:, :]
    for u in range(NU):
        rows = slice(u * UTT, (u + 1) * UTT)
        gated = value[rows, :] * jax.nn.sigmoid(gate[rows, :])
        gated = jnp.where(keep(frames_of[u] // PATCH, (UTT, CB)), gated, 0.0)
        seen = mm(fwd[...], twice(gated))
        a, b = seen[:IM], seen[IM:]
        moved = jnp.concatenate([a * re - b * im, a * im + b * re], axis=0)
        filtered[rows, :] = mm(inv[...], twice(moved))


def block_start(slots, i, flip):
    core = slots[32] if flip == 0 else 1 - slots[32]
    return pl.multiple_of((2 * i + core) * ROWS, 16)


def out_kernel(slots, unused_1, unused_2, unused_3, filtered, mix_grad, second_gain, mine, other, swished, turned, term):
    def ahead(u, carry):
        rows = pl.ds(pl.multiple_of(u * UTT, UTT), UTT)
        unit, unused = normalise(filtered[rows, :])
        z = unit * second_gain[...]
        narrow = (z * jax.nn.sigmoid(z)).astype(BF16)
        swished[rows, :] = narrow
        turned[:, rows] = narrow.T
        return carry

    lax.fori_loop(0, NU, ahead, 0)

    def product(n, carry):
        cols = pl.ds(pl.multiple_of(n * CB, CB), CB)
        term[...] = mm(turned[...], mix_grad[:, cols]).astype(BF16)
        for i in range(16):
            mine[slots[i], :, cols] = term[pl.ds(block_start(slots, i, 0), ROWS), :]
            other[slots[16 + i], :, cols] = term[pl.ds(block_start(slots, i, 1), ROWS), :]
        return carry

    lax.fori_loop(0, NB, product, 0)


def mid_kernel(offsets, *refs):
    pieces, refs = refs[:ND], refs[ND:]
    filtered, mix_grad, second_gain, filter_grad, second_grad, held, sems, back, slope, scales = refs
    copies = assembly(offsets, pieces, held, sems)
    for copy in copies:
        copy.start()
    second_grad[...] = jnp.zeros((1, D), F32)

    def ahead(u, carry):
        rows = pl.ds(pl.multiple_of(u * UTT, UTT), UTT)
        unit, scale = normalise(filtered[rows, :])
        z = unit * second_gain[...]
        sig = jax.nn.sigmoid(z)
        slope[rows, :] = sig * (1.0 + z * (1.0 - sig))
        filter_grad[rows, :] = unit
        scales[rows, :] = jnp.broadcast_to(scale, (UTT, 128))
        return carry

    lax.fori_loop(0, NU, ahead, 0)
    for copy in copies:
        copy.wait()

    def product(n, carry):
        cols = pl.ds(pl.multiple_of(n * 2 * CB, 2 * CB), 2 * CB)
        back[:, cols] = mm_nt(mix_grad[...], held[cols, :])
        return carry

    lax.fori_loop(0, NB // 2, product, 0)

    def behind(u, carry):
        rows = pl.ds(pl.multiple_of(u * UTT, UTT), UTT)
        unit = filter_grad[rows, :]
        dz = back[rows, :] * slope[rows, :]
        second_grad[...] += jnp.sum(dz * unit, axis=0, keepdims=True)
        filter_grad[rows, :] = normalise_back(dz * second_gain[...], unit, scales[rows, :1])
        return carry

    lax.fori_loop(0, NU, behind, 0)


def conv_back_kernel(
    slots, frames_of, unused_1, unused_2, unused_3, value, gate, filter_grad, normed_t, spectrum, fwd, inv_t, fwd_t, ker_t,
    value_grad, gate_grad, mine, other, conv_grad, term,
):
    re, im = spectrum[:IM, :], spectrum[IM:, :]
    sum_re = jnp.zeros((IM, CB), F32)
    sum_im = jnp.zeros((IM, CB), F32)
    for u in range(NU):
        rows = slice(u * UTT, (u + 1) * UTT)
        valid = keep(frames_of[u] // PATCH, (UTT, CB))
        v = value[rows, :]
        sig = jax.nn.sigmoid(gate[rows, :])
        gated = jnp.where(valid, v * sig, 0.0)
        seen = mm(fwd[...], twice(gated))
        a, b = seen[:IM], seen[IM:]
        grad = mm(inv_t[...], twice(filter_grad[rows, :]))
        da, db = grad[:IM], grad[IM:]
        sum_re = sum_re + a * da + b * db
        sum_im = sum_im + a * db - b * da
        spread = jnp.concatenate([re * da + im * db, re * db - im * da], axis=0)
        gated_grad = jnp.where(valid, mm(fwd_t[...], twice(spread)), 0.0)
        part = gated_grad * sig
        value_grad[rows, :] = part.astype(BF16)
        gate_grad[rows, :] = (part * v * (1.0 - sig)).astype(BF16)
    conv_grad[...] = mm(ker_t[...], thrice(jnp.concatenate([sum_re, sum_im], axis=0)))
    for h, grad_ref in enumerate((value_grad, gate_grad)):
        term[...] = mm(normed_t[...], grad_ref[...]).astype(BF16)
        for i in range(16):
            cols = slice(h * CB, (h + 1) * CB)
            mine[slots[i], :, cols] = term[pl.ds(block_start(slots, i, 0), ROWS), :]
            other[slots[16 + i], :, cols] = term[pl.ds(block_start(slots, i, 1), ROWS), :]


def stem_back_kernel(offsets, frames_of, *refs):
    pieces, refs = refs[:NP], refs[NP:]
    grads, refs = refs[:4], refs[4:]
    (unused_1, unused_2, unused_3, embedded, stem_total, mix_grad, first_gain, frames_t,
     first_grad, stem_grad, held, sems, back, pre_grad) = refs
    assemble(offsets, pieces, held, sems)
    first_grad[...] = jnp.zeros((1, D), F32)

    def product(n, carry):
        cols = pl.ds(pl.multiple_of(n * CB, CB), CB)
        total = jnp.zeros((TOK, CB), F32)
        begin = 0
        for grad in grads:
            total = total + mm_nt(grad[...], held[cols, begin : begin + grad.shape[1]])
            begin += grad.shape[1]
        back[:, cols] = total
        return carry

    lax.fori_loop(0, NB, product, 0)

    def behind(u, carry):
        rows = pl.ds(pl.multiple_of(u * UTT, UTT), UTT)
        unit, scale = normalise(embedded[rows, :].astype(F32))
        grad = back[rows, :]
        first_grad[...] += jnp.sum(grad * unit, axis=0, keepdims=True)
        grad = normalise_back(grad * first_gain[...], unit, scale) + mix_grad[rows, :].astype(F32)
        total = stem_total[rows, :]
        sig = jax.nn.sigmoid(total)
        grad = grad * (sig * (1.0 + total * (1.0 - sig)))
        valid = keep(frames_of[u] // PATCH, (UTT, D))
        pre_grad[rows, :] = jnp.where(valid, grad, 0.0).astype(BF16)
        return carry

    lax.fori_loop(0, NU, behind, 0)
    outer = mm(frames_t[...], pre_grad[...])
    outer = jnp.where(stem_masks(TOK, D), outer, 0.0)
    pick = tap_select(TOK).T
    folded = mm(jnp.concatenate([pick, pick], axis=1), split_rows(outer))
    channel = channel_select()
    high = folded.astype(BF16)
    low = (folded - high.astype(F32)).astype(BF16)
    stem_grad[...] = mm_nt(high, channel) + mm_nt(low, channel)


def split_rows(values):
    high = values.astype(BF16)
    low = (values - high.astype(F32)).astype(BF16)
    return jnp.concatenate([high, low], axis=0)


def mixed_kernel(offsets, frames_of, *refs):
    pieces, refs = refs[:ND], refs[ND:]
    unused, swished, embedded, output, held, sems = refs
    assemble(offsets, pieces, held, sems)

    def product(n, carry):
        cols = pl.ds(pl.multiple_of(n * 2 * CB, 2 * CB), 2 * CB)
        mixed = mm(swished[...], held[:, cols])
        for u in range(NU):
            rows = slice(u * UTT, (u + 1) * UTT)
            total = embedded[rows, cols].astype(F32) + mixed[rows]
            valid = keep(frames_of[u] // PATCH, (UTT, 2 * CB))
            output[rows, cols] = jnp.where(valid, total, 0.0).astype(BF16)
        return carry

    lax.fori_loop(0, NB // 2, product, 0)


def chip_sum_kernel(mine_1, other_1, mine_2, other_2, *groups):
    wide = mine_1.shape[-1]
    for r, group in enumerate(groups):
        group[0, :, :wide] = (mine_1[r, 0].astype(F32) + other_1[r, 0].astype(F32)).astype(BF16)
        group[0, :, wide:] = (mine_2[r, 0].astype(F32) + other_2[r, 0].astype(F32)).astype(BF16)


SMEM = pl.BlockSpec(memory_space=pltpu.SMEM)
ANY = pl.BlockSpec(memory_space=pl.ANY)
VMEM = pl.BlockSpec(memory_space=pltpu.VMEM)


def shaped(shape, dtype):
    return jax.ShapeDtypeStruct(shape, dtype)


def call(kernel, name, operands, in_specs, outs, out_specs, scratch, flops, nbytes, vmem, grid=None):
    more = {} if grid is None else {"grid": grid}
    return pl.pallas_call(
        kernel,
        name=name,
        out_shape=outs,
        in_specs=in_specs,
        out_specs=out_specs,
        scratch_shapes=scratch,
        compiler_params=pltpu.CompilerParams(vmem_limit_bytes=vmem * MIB),
        cost_estimate=pl.CostEstimate(flops=flops // COST, bytes_accessed=nbytes // COST, transcendentals=0),
        **more,
    )(*operands)


def stem(before, arrived, frames_of, stem_weight, first_gain, conv_kernel, cotangent, tables):
    outs = [
        shaped((TOK, D), F32), shaped((TOK, D), BF16), shaped((TOK, D), BF16), shaped((D, TOK), BF16),
        shaped((TOK, TOK), BF16), shaped((SPEC, D), F32), shaped((TOK, D), BF16),
    ]
    return call(
        stem_kernel, "stem",
        (before, frames_of, arrived, stem_weight, first_gain, conv_kernel, cotangent, tables["ker"]),
        [ANY, SMEM] + [VMEM] * 6, outs, [VMEM] * 7,
        [pltpu.VMEM((TOK * PATCH, MEL), F32), pltpu.VMEM((TOK, D), BF16)],
        2 * TOK * TOK * D, 14 * MIB, 26,
    )


def gate_forward(offsets, frames_of, pieces, normed, spectrum, tables):
    whole = lambda n: (0, 0)
    block = lambda n: (0, n)
    return call(
        gate_kernel, "gate",
        (offsets, frames_of, *pieces, normed, spectrum, tables["fwd"], tables["inv"]),
        [SMEM, SMEM] + [ANY] * NP
        + [pl.BlockSpec((TOK, D), whole), pl.BlockSpec((SPEC, CB), block),
           pl.BlockSpec(tables["fwd"].shape, whole), pl.BlockSpec(tables["inv"].shape, whole)],
        [shaped((TOK, D), F32)] * 3, [pl.BlockSpec((TOK, CB), block)] * 3,
        [pltpu.VMEM((D, 2 * D), BF16), pltpu.SemaphoreType.DMA((32,))],
        2 * TOK * D * 2 * D, 22 * MIB, 26, grid=(NB,),
    )


def out_grad(slots, before, filtered, mix_grad, second_gain):
    half = shaped((16, ROWS, D), BF16)
    return call(
        out_kernel, "out_grad", (slots, *before, filtered, mix_grad, second_gain),
        [SMEM] + [ANY] * 3 + [VMEM] * 3, [half, half, shaped((TOK, D), BF16)], [VMEM] * 3,
        [pltpu.VMEM((D, TOK), BF16), pltpu.VMEM((D, CB), BF16)],
        16 * 2 * TOK * D * D, 16 * 11 * MIB, 24,
    )


def middle(offsets, pieces, filtered, mix_grad, second_gain):
    return call(
        mid_kernel, "middle", (offsets, *pieces, filtered, mix_grad, second_gain),
        [SMEM] + [ANY] * ND + [VMEM] * 3, [shaped((TOK, D), F32), shaped((1, D), F32)], [VMEM] * 2,
        [pltpu.VMEM((D, D), BF16), pltpu.SemaphoreType.DMA((32,)), pltpu.VMEM((TOK, D), F32),
         pltpu.VMEM((TOK, D), F32), pltpu.VMEM((TOK, 128), F32)],
        16 * 2 * TOK * D * D, 16 * 13 * MIB, 28,
    )


def conv_back(slots, frames_of, before, value, gate, filter_grad, normed_t, spectrum, tables, begin, count):
    whole = lambda n: (0, 0)
    block = lambda n: (0, n + begin)
    own = lambda n: (0, n)
    width = count * CB
    names = ("fwd", "inv_t", "fwd_t", "ker_t")
    half = shaped((16, ROWS, 2 * width), BF16)
    half_spec = pl.BlockSpec((16, ROWS, 2 * CB), lambda n: (0, 0, n))
    outs = [shaped((TOK, width), BF16), shaped((TOK, width), BF16), half, half, shaped((32, width), F32)]
    return call(
        conv_back_kernel, "conv_back",
        (slots, frames_of, *before, value, gate, filter_grad, normed_t, spectrum, *[tables[k] for k in names]),
        [SMEM, SMEM, ANY, ANY, ANY] + [pl.BlockSpec((TOK, CB), block)] * 3
        + [pl.BlockSpec((D, TOK), whole), pl.BlockSpec((SPEC, CB), block)]
        + [pl.BlockSpec(tables[k].shape, whole) for k in names],
        outs,
        [pl.BlockSpec((TOK, CB), own)] * 2 + [half_spec, half_spec, pl.BlockSpec((32, CB), own)],
        [pltpu.VMEM((D, CB), BF16)], 2 * TOK * D * width * 2 * 16, 22 * MIB * count // NB * 16, 22, grid=(count,),
    )


def stem_back(offsets, frames_of, pieces, grads, before, embedded, stem_total, mix_grad, first_gain, frames_t):
    return call(
        stem_back_kernel, "stem_back",
        (offsets, frames_of, *pieces, *grads, *before, embedded, stem_total, mix_grad, first_gain, frames_t),
        [SMEM, SMEM] + [ANY] * NP + [VMEM] * 4 + [ANY] * 3 + [VMEM] * 5,
        [shaped((1, D), F32), shaped((16, CH), F32)], [VMEM] * 2,
        [pltpu.VMEM((D, 2 * D), BF16), pltpu.SemaphoreType.DMA((32,)), pltpu.VMEM((TOK, D), F32), pltpu.VMEM((TOK, D), BF16)],
        16 * 2 * TOK * D * 2 * D, 16 * 20 * MIB, 36,
    )


def mixed_out(offsets, frames_of, pieces, before, swished, embedded):
    return call(
        mixed_kernel, "mixed",
        (offsets, frames_of, *pieces, before, swished, embedded),
        [SMEM, SMEM] + [ANY] * (ND + 1) + [VMEM] * 2,
        shaped((TOK, D), BF16), VMEM,
        [pltpu.VMEM((D, D), BF16), pltpu.SemaphoreType.DMA((32,))],
        2 * TOK * D * D, 10 * MIB, 18,
    )


def chip_sums(parts):
    operands = [value.reshape(4, 4, *value.shape[1:]) for part in parts for value in part]
    width = 2 * D
    spec = lambda value: pl.BlockSpec((4, 1, *value.shape[2:]), lambda m: (0, m, 0, 0))
    return call(
        chip_sum_kernel, "chip_sum", operands, [spec(value) for value in operands],
        [shaped((4, ROWS, width), BF16)] * 4, [pl.BlockSpec((1, ROWS, width), lambda m: (m, 0, 0))] * 4,
        [], 16 * ROWS * width, 14 * MIB, 18, grid=(4,),
    )


def place(x, y, z, c):
    return ((x % 4 * 4 + y % 4) * 4 + z % 4) * 2 + c


def pairs(step):
    found = []
    for x in range(4):
        for y in range(4):
            for z in range(4):
                for c in range(2):
                    found.append((place(x, y, z, c), step(x, y, z, c)))
    return found


def along_first(r):
    return pairs(lambda x, y, z, c: place(x, y ^ (r * c), z ^ (r * (1 - c)), c))


def along_second(r):
    return pairs(lambda x, y, z, c: place(x, y ^ (r * (1 - c)), z ^ (r * c), c))


def along_x(r):
    return pairs(lambda x, y, z, c: place(x ^ r, y, z, c))


def other_core():
    return pairs(lambda x, y, z, c: place(x, y, z, 1 - c))


def send(values, where):
    return lax.ppermute(values, ALL, where)


def gather_offsets(y, z, c):
    m, j = np.divmod(np.arange(16, dtype=np.int32), 4)

    def of(core):
        row_y = y ^ jnp.where(core == 0, m, j)
        row_z = z ^ jnp.where(core == 0, j, m)
        return ((row_y * 4 + row_z) * 2 + core) * ROWS

    return jnp.concatenate([of(c), of(1 - c)]).astype(jnp.int32)


def scatter_slots(y, z, c):
    block = np.arange(16, dtype=np.int32)
    far_y, far_z = (block // 4) ^ y, (block % 4) ^ z

    def of(core):
        return jnp.where(core == 0, far_z * 4 + far_y, far_y * 4 + far_z)

    return jnp.concatenate([of(c), of(1 - c), c[None]]).astype(jnp.int32)


def zero_of(values):
    return values[(0,) * values.ndim] * 0


def gather_near(shard):
    return jnp.stack([shard] + [send(shard, along_first(r)) for r in (1, 2, 3)])


def gather_far(near):
    halves = near[:2], near[2:]
    first = [send(half, along_second(r)) for half, r in zip(halves, (1, 3))]
    second = [
        send(jnp.stack([half, got]), along_second(r)) for half, got, r in zip(halves, first, (3, 1))
    ]
    return first, second


def gather_pieces(near, first, second, after):
    own = [near, first[0], first[1], second[0].reshape(4, *near.shape[1:]), second[1].reshape(4, *near.shape[1:])]
    return own + [send(piece + after, other_core()) for piece in own]


def gather_direct(near):
    return [near] + [send(near, along_second(r)) for r in (1, 2, 3)]


def with_other(own, after):
    return own + [send(piece + after if i else piece, other_core()) for i, piece in enumerate(own)]


DIRECT = tuple(tuple((r, j) for j in range(4)) for r in range(4))
PIECES = (
    ((0, 0), (0, 1), (0, 2), (0, 3)),
    ((1, 0), (1, 1)),
    ((3, 2), (3, 3)),
    ((3, 0), (3, 1), (2, 0), (2, 1)),
    ((1, 2), (1, 3), (2, 2), (2, 3)),
)
NP = 2 * len(PIECES)
ND = 2 * len(DIRECT)


def total_of(parts):
    summed = parts[0].astype(F32)
    for part in parts[1:]:
        summed = summed + part.astype(F32)
    return summed


def chip_sum(mine, other):
    other = send(other, other_core())
    return [total_of([mine[4 * j : 4 * j + 4], other[4 * j : 4 * j + 4]]).astype(BF16) for j in range(4)]


def scatter_first(groups):
    return [groups[0]] + [send(groups[r], along_first(r)) for r in (1, 2, 3)]


def scatter_rest(near, follow):
    close = total_of([near[0]] + [send(near[r], along_second(r)) for r in (1, 2, 3)]) + follow
    close = close.astype(BF16)
    wide = close.shape[1] // 2
    halves = []
    for half, order in ((close[:, :wide], (1, 3)), (close[:, wide:], (3, 1))):
        half = total_of([half, send(half, along_x(order[0]))]).astype(BF16)
        halves.append(total_of([half, send(half, along_x(order[1]))]))
    return jnp.concatenate(halves, axis=1)


def half_of_chip(values, c):
    return jnp.where(c == 0, values[0], values[1]) + send(jnp.where(c == 0, values[1], values[0]), other_core())


def finish_small(values, rows, c):
    narrow = values.astype(BF16)
    values = total_of([values] + [send(narrow, along_first(r)) for r in (1, 2, 3)])
    other = send(values, other_core())
    mine, late = values[:rows], values[rows:] + other[rows:]
    other = other[:rows]
    return jnp.concatenate([jnp.where(c == 0, mine, other), jnp.where(c == 0, other, mine)]), late


def body(
    tables, log_mel, bucket_list, utterance_frames, stem_weight, first_gain, gate_proj, conv_kernel, second_gain,
    out_proj, cotangent,
):
    y, z, c = lax.axis_index("y"), lax.axis_index("z"), lax.axis_index("c")
    offsets = gather_offsets(y, z, c)
    slots = scatter_slots(y, z, c)
    tables = {name: jnp.asarray(value) for name, value in tables.items()}
    first_gain, second_gain = first_gain[None], second_gain[None]

    gate_near = gather_near(gate_proj)
    outgoing = jnp.take(log_mel, bucket_list[0], axis=0) + zero_of(gate_near[1])
    arrived = lax.all_to_all(outgoing, ALL, split_axis=0, concat_axis=0, tiled=True)
    gate_far = gather_far(gate_near)
    stem_total, embedded, normed, normed_t, frames_t, spectrum, mix_grad = stem(
        gate_far[0][0], arrived.reshape(TOK * PATCH, MEL), utterance_frames, stem_weight, first_gain, conv_kernel, cotangent, tables
    )
    gate_pieces = gather_pieces(gate_near, *gate_far, zero_of(normed))
    out_near = gather_near(out_proj + zero_of(gate_far[0][0])) + sum(zero_of(piece) for piece in gate_far[1])
    out_own = gather_direct(out_near)
    value, gate, filtered = gate_forward(offsets, utterance_frames, gate_pieces, normed, spectrum, tables)
    out_pieces = with_other(out_own, zero_of(filtered).astype(BF16))
    out_mine, out_other, swished = out_grad(slots, out_own[1:], filtered, mix_grad, second_gain)
    filter_grad, second_grad = middle(offsets, out_pieces, filtered, mix_grad, second_gain)
    out_sums = chip_sum(out_mine, out_other)
    out_groups = scatter_first(out_sums)
    grads, nears, convs = [], [], []
    for begin, count in ((0, 4), (4, 2)):
        value_grad, gate_grad, mine, other, conv_grad = conv_back(
            slots, utterance_frames, out_sums[1:], value, gate, filter_grad, normed_t, spectrum, tables, begin, count
        )
        grads.append((value_grad, gate_grad))
        if begin:
            other = other + sum(zero_of(group) for group in out_groups[1:])
        nears.append((mine, send(other, other_core())))
        convs.append(conv_grad[:TAPS])
    gate_groups = chip_sums(nears)
    first_grad, stem_grad = stem_back(
        offsets, utterance_frames, gate_pieces, [pair[k] for k in range(2) for pair in grads], gate_groups[1:], embedded,
        stem_total, mix_grad, first_gain, frames_t,
    )
    early = jnp.concatenate([jnp.concatenate(convs, axis=1), second_grad], axis=0)
    early = half_of_chip(early.reshape(2, 16, D), c)
    follow = zero_of(first_grad)
    terms = [scatter_first(gate_groups), out_groups]
    near = jnp.concatenate([(total_of(term) + follow).astype(BF16) for term in terms], axis=-1)
    late = jnp.concatenate([first_grad, jnp.pad(stem_grad.reshape(1, -1), ((0, 0), (0, D - 16 * CH)))], axis=0)
    small = jnp.concatenate([early, late, jnp.zeros((6, D), F32)], axis=0)
    small = jnp.concatenate([small[:8], small[8:16], small[16:]], axis=1).astype(BF16)
    near = jnp.concatenate([near, jnp.broadcast_to(small[None], (4, *small.shape))], axis=1)
    output = mixed_out(offsets, utterance_frames, out_pieces, near, swished, embedded)
    sums = scatter_rest(near, zero_of(output).astype(F32))
    small = sums[ROWS:]
    early, late = finish_small(
        jnp.concatenate([small[:, :D], small[:, D : 2 * D], small[:2, 2 * D :]]), 16, c
    )
    sums = sums[:ROWS]
    blocks = [sums[:, i * CB : (i + 1) * CB] for i in range(2 * NB)]
    gate_sums = jnp.concatenate(blocks[::2] + blocks[1::2], axis=1)
    return (
        output, gate_sums, sums[:, 2 * D :], late[1, : 16 * CH].reshape(16, CH), late[0],
        early[:TAPS], early[TAPS],
    )


def solution(mesh):
    grid = Mesh(mesh.devices.reshape(4, 4, 4, 2), ALL)
    rows = ("y", "z", "c")
    return jax.shard_map(
        functools.partial(body, transforms()),
        mesh=grid,
        in_specs=(
            P(ALL, None, None), P(ALL, None), P(ALL), P(), P(), P(rows, None), P(), P(), P(rows, None), P(ALL, None),
        ),
        out_specs=(P(ALL, None), P(rows, None), P(rows, None), P(), P(), P(), P()),
        check_vma=False,
    )
```

```python
import functools

import jax
import jax.numpy as jnp
import numpy as np
from jax import lax
from jax.experimental import pallas as pl
from jax.experimental.pallas import tpu as pltpu
from jax.sharding import Mesh
from jax.sharding import PartitionSpec as P

PATCH = 4
UTT = 128
TOK = 512
NU = TOK // UTT
D = 1536
MEL = 128
CH = 48
TAPS = 31
HALF = TAPS // 2
EPS = 1e-05
ROWS = 48
CB = 256
NB = D // CB
ALL = ("x", "y", "z", "c")
F32 = jnp.float32
BF16 = jnp.bfloat16
MIB = 1024 * 1024
COST = 1

CYC = 144
BINS = CYC // 2 + 1
IM = 80
SPEC = 160


def hi_lo(values):
    high = values.astype(np.float32).astype(jnp.bfloat16)
    low = (values - high.astype(np.float64)).astype(np.float32).astype(jnp.bfloat16)
    return high, low


def side_by_side(values, three=False):
    high, low = hi_lo(values)
    parts = [high, low] + ([high] if three else [])
    return np.concatenate(parts, axis=1)


def transforms():
    angle = 2 * np.pi / CYC
    bins = np.arange(BINS)[:, None]
    places = np.arange(UTT)[None, :]
    offsets = np.arange(TAPS)[None, :] - HALF
    forward = np.zeros((SPEC, UTT))
    forward[:BINS] = np.cos(angle * bins * places)
    forward[IM : IM + BINS] = -np.sin(angle * bins * places)
    kernel = np.zeros((SPEC, 32))
    kernel[:BINS, :TAPS] = np.cos(angle * bins * offsets)
    kernel[IM : IM + BINS, :TAPS] = np.sin(angle * bins * offsets)
    weight = np.full((BINS, 1), 2.0 / CYC)
    weight[0] = weight[-1] = 1.0 / CYC
    back = np.zeros((UTT, SPEC))
    back[:, :BINS] = (weight * np.cos(angle * bins * places)).T
    back[:, IM : IM + BINS] = -(weight * np.sin(angle * bins * places)).T
    return {
        "fwd": side_by_side(forward),
        "inv": side_by_side(back),
        "fwd_t": side_by_side(forward.T),
        "inv_t": side_by_side(back.T),
        "ker": side_by_side(kernel, True),
        "ker_t": side_by_side(kernel.T, True),
    }


def twice(values):
    narrow = values.astype(BF16)
    return jnp.concatenate([narrow, narrow], axis=0)


def thrice(values):
    high = values.astype(BF16)
    low = (values - high.astype(F32)).astype(BF16)
    return jnp.concatenate([high, high, low], axis=0)


def mm(left, right):
    return jnp.dot(left, right, preferred_element_type=F32)


def mm_nt(left, right):
    return lax.dot_general(left, right, (((1,), (1,)), ((), ())), preferred_element_type=F32)


def keep(limit, shape):
    return lax.broadcasted_iota(jnp.int32, shape, 0) < limit


def row_mean(values):
    return jnp.sum(values, axis=-1, keepdims=True) * (1.0 / D)


def normalise(values):
    centred = values - row_mean(values)
    scale = lax.rsqrt(row_mean(centred * centred) + EPS)
    return centred * scale, scale


def normalise_back(grad, unit, scale):
    return scale * (grad - row_mean(grad) - unit * row_mean(grad * unit))


def stem_masks(rows, cols):
    row = lax.broadcasted_iota(jnp.int32, (rows, cols), 0)
    col = lax.broadcasted_iota(jnp.int32, (rows, cols), 1)
    group = (row % MEL) // PATCH
    first = group * CH
    return (col >= first) & (col < first + CH)


def tap_select(rows):
    row = lax.broadcasted_iota(jnp.int32, (rows, 16), 0)
    tap = lax.broadcasted_iota(jnp.int32, (rows, 16), 1)
    return (tap == PATCH * (row // MEL) + row % PATCH).astype(F32).astype(BF16)


def channel_select():
    row = lax.broadcasted_iota(jnp.int32, (CH, D), 0)
    col = lax.broadcasted_iota(jnp.int32, (CH, D), 1)
    return (col % CH == row).astype(F32).astype(BF16)


def stem_kernel(
    unused, frames_of, arrived, stem_weight, first_gain, conv_kernel, cotangent, ker,
    stem_total, embedded, normed, normed_t, frames_t, spectrum, mix_grad, wide, big,
):
    wide[...] = arrived[...].astype(F32)
    taps = mm(tap_select(TOK), stem_weight[...]).astype(BF16)
    spread = mm(taps, channel_select())
    big[...] = jnp.where(stem_masks(TOK, D), spread, 0.0).astype(BF16)
    padded = jnp.concatenate([conv_kernel[...], jnp.zeros((1, D), F32)], axis=0)
    spectrum[...] = mm(ker[...], thrice(padded))

    def one(u, carry):
        base = pl.multiple_of(u * UTT, UTT)
        rows = pl.ds(base, UTT)
        parts = [wide[pl.ds(base * PATCH + i, UTT, stride=PATCH), :].astype(BF16) for i in range(PATCH)]
        frames = jnp.concatenate(parts, axis=1)
        total = mm(frames, big[...])
        stem_total[rows, :] = total
        valid = keep(frames_of[u] // PATCH, (UTT, D))
        kept = jnp.where(valid, total * jax.nn.sigmoid(total), 0.0).astype(BF16)
        embedded[rows, :] = kept
        unit, scale = normalise(kept.astype(F32))
        narrow = (unit * first_gain[...]).astype(BF16)
        normed[rows, :] = narrow
        normed_t[:, rows] = narrow.T
        frames_t[:, rows] = frames.T
        mix_grad[rows, :] = jnp.where(valid, cotangent[rows, :].astype(F32), 0.0).astype(BF16)
        return carry

    lax.fori_loop(0, NU, one, 0)


def assembly(offsets, pieces, held, sems):
    copies = []
    layout = PIECES if len(pieces) == NP else DIRECT
    for p, piece in enumerate(pieces):
        for j, (second, first) in enumerate(layout[p % len(layout)]):
            block = p // len(layout) * 16 + second * 4 + first
            start = pl.multiple_of(offsets[block], 16)
            copies.append(pltpu.make_async_copy(piece.at[j], held.at[pl.ds(start, ROWS), :], sems.at[block]))
    return copies


def assemble(offsets, pieces, held, sems):
    copies = assembly(offsets, pieces, held, sems)
    for copy in copies:
        copy.start()
    for copy in copies:
        copy.wait()


def gate_kernel(offsets, frames_of, *refs):
    pieces, refs = refs[:NP], refs[NP:]
    normed, spectrum, fwd, inv, value, gate, filtered, held, sems = refs
    n = pl.program_id(0)

    @pl.when(n == 0)
    def _():
        assemble(offsets, pieces, held, sems)

    start = pl.multiple_of(n * CB, CB)
    value[...] = mm(normed[...], held[:, pl.ds(start, CB)])
    gate[...] = mm(normed[...], held[:, pl.ds(pl.multiple_of(D + start, CB), CB)])
    re, im = spectrum[:IM, :], spectrum[IM:, :]
    for u in range(NU):
        rows = slice(u * UTT, (u + 1) * UTT)
        gated = value[rows, :] * jax.nn.sigmoid(gate[rows, :])
        gated = jnp.where(keep(frames_of[u] // PATCH, (UTT, CB)), gated, 0.0)
        seen = mm(fwd[...], twice(gated))
        a, b = seen[:IM], seen[IM:]
        moved = jnp.concatenate([a * re - b * im, a * im + b * re], axis=0)
        filtered[rows, :] = mm(inv[...], twice(moved))


def block_start(slots, i, flip):
    core = slots[32] if flip == 0 else 1 - slots[32]
    return pl.multiple_of((2 * i + core) * ROWS, 16)


def out_kernel(slots, unused_1, unused_2, unused_3, filtered, mix_grad, second_gain, mine, other, swished, turned, term):
    def ahead(u, carry):
        rows = pl.ds(pl.multiple_of(u * UTT, UTT), UTT)
        unit, unused = normalise(filtered[rows, :])
        z = unit * second_gain[...]
        narrow = (z * jax.nn.sigmoid(z)).astype(BF16)
        swished[rows, :] = narrow
        turned[:, rows] = narrow.T
        return carry

    lax.fori_loop(0, NU, ahead, 0)

    def product(n, carry):
        cols = pl.ds(pl.multiple_of(n * CB, CB), CB)
        term[...] = mm(turned[...], mix_grad[:, cols]).astype(BF16)
        for i in range(16):
            mine[slots[i], :, cols] = term[pl.ds(block_start(slots, i, 0), ROWS), :]
            other[slots[16 + i], :, cols] = term[pl.ds(block_start(slots, i, 1), ROWS), :]
        return carry

    lax.fori_loop(0, NB, product, 0)


def mid_kernel(offsets, *refs):
    pieces, refs = refs[:ND], refs[ND:]
    filtered, mix_grad, second_gain, filter_grad, second_grad, held, sems, back, slope, scales = refs
    copies = assembly(offsets, pieces, held, sems)
    for copy in copies:
        copy.start()
    second_grad[...] = jnp.zeros((1, D), F32)

    def ahead(u, carry):
        rows = pl.ds(pl.multiple_of(u * UTT, UTT), UTT)
        unit, scale = normalise(filtered[rows, :])
        z = unit * second_gain[...]
        sig = jax.nn.sigmoid(z)
        slope[rows, :] = sig * (1.0 + z * (1.0 - sig))
        filter_grad[rows, :] = unit
        scales[rows, :] = jnp.broadcast_to(scale, (UTT, 128))
        return carry

    lax.fori_loop(0, NU, ahead, 0)
    for copy in copies:
        copy.wait()

    def product(n, carry):
        cols = pl.ds(pl.multiple_of(n * 2 * CB, 2 * CB), 2 * CB)
        back[:, cols] = mm_nt(mix_grad[...], held[cols, :])
        return carry

    lax.fori_loop(0, NB // 2, product, 0)

    def behind(u, carry):
        rows = pl.ds(pl.multiple_of(u * UTT, UTT), UTT)
        unit = filter_grad[rows, :]
        dz = back[rows, :] * slope[rows, :]
        second_grad[...] += jnp.sum(dz * unit, axis=0, keepdims=True)
        filter_grad[rows, :] = normalise_back(dz * second_gain[...], unit, scales[rows, :1])
        return carry

    lax.fori_loop(0, NU, behind, 0)


def conv_back_kernel(
    slots, frames_of, unused_1, unused_2, unused_3, value, gate, filter_grad, normed_t, spectrum, fwd, inv_t, fwd_t, ker_t,
    value_grad, gate_grad, mine, other, conv_grad, term,
):
    re, im = spectrum[:IM, :], spectrum[IM:, :]
    sum_re = jnp.zeros((IM, CB), F32)
    sum_im = jnp.zeros((IM, CB), F32)
    for u in range(NU):
        rows = slice(u * UTT, (u + 1) * UTT)
        valid = keep(frames_of[u] // PATCH, (UTT, CB))
        v = value[rows, :]
        sig = jax.nn.sigmoid(gate[rows, :])
        gated = jnp.where(valid, v * sig, 0.0)
        seen = mm(fwd[...], twice(gated))
        a, b = seen[:IM], seen[IM:]
        grad = mm(inv_t[...], twice(filter_grad[rows, :]))
        da, db = grad[:IM], grad[IM:]
        sum_re = sum_re + a * da + b * db
        sum_im = sum_im + a * db - b * da
        spread = jnp.concatenate([re * da + im * db, re * db - im * da], axis=0)
        gated_grad = jnp.where(valid, mm(fwd_t[...], twice(spread)), 0.0)
        part = gated_grad * sig
        value_grad[rows, :] = part.astype(BF16)
        gate_grad[rows, :] = (part * v * (1.0 - sig)).astype(BF16)
    conv_grad[...] = mm(ker_t[...], thrice(jnp.concatenate([sum_re, sum_im], axis=0)))
    for h, grad_ref in enumerate((value_grad, gate_grad)):
        term[...] = mm(normed_t[...], grad_ref[...]).astype(BF16)
        for i in range(16):
            cols = slice(h * CB, (h + 1) * CB)
            mine[slots[i], :, cols] = term[pl.ds(block_start(slots, i, 0), ROWS), :]
            other[slots[16 + i], :, cols] = term[pl.ds(block_start(slots, i, 1), ROWS), :]


def stem_back_kernel(offsets, frames_of, *refs):
    pieces, refs = refs[:NP], refs[NP:]
    grads, refs = refs[:4], refs[4:]
    (unused_1, unused_2, unused_3, embedded, stem_total, mix_grad, first_gain, frames_t,
     first_grad, stem_grad, held, sems, back, pre_grad) = refs
    assemble(offsets, pieces, held, sems)
    first_grad[...] = jnp.zeros((1, D), F32)

    def product(n, carry):
        cols = pl.ds(pl.multiple_of(n * CB, CB), CB)
        total = jnp.zeros((TOK, CB), F32)
        begin = 0
        for grad in grads:
            total = total + mm_nt(grad[...], held[cols, begin : begin + grad.shape[1]])
            begin += grad.shape[1]
        back[:, cols] = total
        return carry

    lax.fori_loop(0, NB, product, 0)

    def behind(u, carry):
        rows = pl.ds(pl.multiple_of(u * UTT, UTT), UTT)
        unit, scale = normalise(embedded[rows, :].astype(F32))
        grad = back[rows, :]
        first_grad[...] += jnp.sum(grad * unit, axis=0, keepdims=True)
        grad = normalise_back(grad * first_gain[...], unit, scale) + mix_grad[rows, :].astype(F32)
        total = stem_total[rows, :]
        sig = jax.nn.sigmoid(total)
        grad = grad * (sig * (1.0 + total * (1.0 - sig)))
        valid = keep(frames_of[u] // PATCH, (UTT, D))
        pre_grad[rows, :] = jnp.where(valid, grad, 0.0).astype(BF16)
        return carry

    lax.fori_loop(0, NU, behind, 0)
    outer = mm(frames_t[...], pre_grad[...])
    outer = jnp.where(stem_masks(TOK, D), outer, 0.0)
    pick = tap_select(TOK).T
    folded = mm(jnp.concatenate([pick, pick], axis=1), split_rows(outer))
    channel = channel_select()
    high = folded.astype(BF16)
    low = (folded - high.astype(F32)).astype(BF16)
    stem_grad[...] = mm_nt(high, channel) + mm_nt(low, channel)


def split_rows(values):
    high = values.astype(BF16)
    low = (values - high.astype(F32)).astype(BF16)
    return jnp.concatenate([high, low], axis=0)


def mixed_kernel(offsets, frames_of, *refs):
    pieces, refs = refs[:ND], refs[ND:]
    unused, swished, embedded, output, held, sems = refs
    assemble(offsets, pieces, held, sems)

    def product(n, carry):
        cols = pl.ds(pl.multiple_of(n * 2 * CB, 2 * CB), 2 * CB)
        mixed = mm(swished[...], held[:, cols])
        for u in range(NU):
            rows = slice(u * UTT, (u + 1) * UTT)
            total = embedded[rows, cols].astype(F32) + mixed[rows]
            valid = keep(frames_of[u] // PATCH, (UTT, 2 * CB))
            output[rows, cols] = jnp.where(valid, total, 0.0).astype(BF16)
        return carry

    lax.fori_loop(0, NB // 2, product, 0)


def chip_sum_kernel(mine_1, other_1, mine_2, other_2, *groups):
    wide = mine_1.shape[-1]
    for r, group in enumerate(groups):
        group[0, :, :wide] = (mine_1[r, 0].astype(F32) + other_1[r, 0].astype(F32)).astype(BF16)
        group[0, :, wide:] = (mine_2[r, 0].astype(F32) + other_2[r, 0].astype(F32)).astype(BF16)


SMEM = pl.BlockSpec(memory_space=pltpu.SMEM)
ANY = pl.BlockSpec(memory_space=pl.ANY)
VMEM = pl.BlockSpec(memory_space=pltpu.VMEM)


def shaped(shape, dtype):
    return jax.ShapeDtypeStruct(shape, dtype)


def call(kernel, name, operands, in_specs, outs, out_specs, scratch, flops, nbytes, vmem, grid=None):
    more = {} if grid is None else {"grid": grid}
    return pl.pallas_call(
        kernel,
        name=name,
        out_shape=outs,
        in_specs=in_specs,
        out_specs=out_specs,
        scratch_shapes=scratch,
        compiler_params=pltpu.CompilerParams(vmem_limit_bytes=vmem * MIB),
        cost_estimate=pl.CostEstimate(flops=flops // COST, bytes_accessed=nbytes // COST, transcendentals=0),
        **more,
    )(*operands)


def stem(before, arrived, frames_of, stem_weight, first_gain, conv_kernel, cotangent, tables):
    outs = [
        shaped((TOK, D), F32), shaped((TOK, D), BF16), shaped((TOK, D), BF16), shaped((D, TOK), BF16),
        shaped((TOK, TOK), BF16), shaped((SPEC, D), F32), shaped((TOK, D), BF16),
    ]
    return call(
        stem_kernel, "stem",
        (before, frames_of, arrived, stem_weight, first_gain, conv_kernel, cotangent, tables["ker"]),
        [ANY, SMEM] + [VMEM] * 6, outs, [VMEM] * 7,
        [pltpu.VMEM((TOK * PATCH, MEL), F32), pltpu.VMEM((TOK, D), BF16)],
        2 * TOK * TOK * D, 14 * MIB, 26,
    )


def gate_forward(offsets, frames_of, pieces, normed, spectrum, tables):
    whole = lambda n: (0, 0)
    block = lambda n: (0, n)
    return call(
        gate_kernel, "gate",
        (offsets, frames_of, *pieces, normed, spectrum, tables["fwd"], tables["inv"]),
        [SMEM, SMEM] + [ANY] * NP
        + [pl.BlockSpec((TOK, D), whole), pl.BlockSpec((SPEC, CB), block),
           pl.BlockSpec(tables["fwd"].shape, whole), pl.BlockSpec(tables["inv"].shape, whole)],
        [shaped((TOK, D), F32)] * 3, [pl.BlockSpec((TOK, CB), block)] * 3,
        [pltpu.VMEM((D, 2 * D), BF16), pltpu.SemaphoreType.DMA((32,))],
        2 * TOK * D * 2 * D, 22 * MIB, 26, grid=(NB,),
    )


def out_grad(slots, before, filtered, mix_grad, second_gain):
    half = shaped((16, ROWS, D), BF16)
    return call(
        out_kernel, "out_grad", (slots, *before, filtered, mix_grad, second_gain),
        [SMEM] + [ANY] * 3 + [VMEM] * 3, [half, half, shaped((TOK, D), BF16)], [VMEM] * 3,
        [pltpu.VMEM((D, TOK), BF16), pltpu.VMEM((D, CB), BF16)],
        16 * 2 * TOK * D * D, 16 * 11 * MIB, 24,
    )


def middle(offsets, pieces, filtered, mix_grad, second_gain):
    return call(
        mid_kernel, "middle", (offsets, *pieces, filtered, mix_grad, second_gain),
        [SMEM] + [ANY] * ND + [VMEM] * 3, [shaped((TOK, D), F32), shaped((1, D), F32)], [VMEM] * 2,
        [pltpu.VMEM((D, D), BF16), pltpu.SemaphoreType.DMA((32,)), pltpu.VMEM((TOK, D), F32),
         pltpu.VMEM((TOK, D), F32), pltpu.VMEM((TOK, 128), F32)],
        16 * 2 * TOK * D * D, 16 * 13 * MIB, 28,
    )


def conv_back(slots, frames_of, before, value, gate, filter_grad, normed_t, spectrum, tables, begin, count):
    whole = lambda n: (0, 0)
    block = lambda n: (0, n + begin)
    own = lambda n: (0, n)
    width = count * CB
    names = ("fwd", "inv_t", "fwd_t", "ker_t")
    half = shaped((16, ROWS, 2 * width), BF16)
    half_spec = pl.BlockSpec((16, ROWS, 2 * CB), lambda n: (0, 0, n))
    outs = [shaped((TOK, width), BF16), shaped((TOK, width), BF16), half, half, shaped((32, width), F32)]
    return call(
        conv_back_kernel, "conv_back",
        (slots, frames_of, *before, value, gate, filter_grad, normed_t, spectrum, *[tables[k] for k in names]),
        [SMEM, SMEM, ANY, ANY, ANY] + [pl.BlockSpec((TOK, CB), block)] * 3
        + [pl.BlockSpec((D, TOK), whole), pl.BlockSpec((SPEC, CB), block)]
        + [pl.BlockSpec(tables[k].shape, whole) for k in names],
        outs,
        [pl.BlockSpec((TOK, CB), own)] * 2 + [half_spec, half_spec, pl.BlockSpec((32, CB), own)],
        [pltpu.VMEM((D, CB), BF16)], 2 * TOK * D * width * 2 * 16, 22 * MIB * count // NB * 16, 22, grid=(count,),
    )


def stem_back(offsets, frames_of, pieces, grads, before, embedded, stem_total, mix_grad, first_gain, frames_t):
    return call(
        stem_back_kernel, "stem_back",
        (offsets, frames_of, *pieces, *grads, *before, embedded, stem_total, mix_grad, first_gain, frames_t),
        [SMEM, SMEM] + [ANY] * NP + [VMEM] * 4 + [ANY] * 3 + [VMEM] * 5,
        [shaped((1, D), F32), shaped((16, CH), F32)], [VMEM] * 2,
        [pltpu.VMEM((D, 2 * D), BF16), pltpu.SemaphoreType.DMA((32,)), pltpu.VMEM((TOK, D), F32), pltpu.VMEM((TOK, D), BF16)],
        16 * 2 * TOK * D * 2 * D, 16 * 20 * MIB, 36,
    )


def mixed_out(offsets, frames_of, pieces, before, swished, embedded):
    return call(
        mixed_kernel, "mixed",
        (offsets, frames_of, *pieces, before, swished, embedded),
        [SMEM, SMEM] + [ANY] * (ND + 1) + [VMEM] * 2,
        shaped((TOK, D), BF16), VMEM,
        [pltpu.VMEM((D, D), BF16), pltpu.SemaphoreType.DMA((32,))],
        2 * TOK * D * D, 10 * MIB, 18,
    )


def chip_sums(parts):
    operands = [value.reshape(4, 4, *value.shape[1:]) for part in parts for value in part]
    width = 2 * D
    spec = lambda value: pl.BlockSpec((4, 1, *value.shape[2:]), lambda m: (0, m, 0, 0))
    return call(
        chip_sum_kernel, "chip_sum", operands, [spec(value) for value in operands],
        [shaped((4, ROWS, width), BF16)] * 4, [pl.BlockSpec((1, ROWS, width), lambda m: (m, 0, 0))] * 4,
        [], 16 * ROWS * width, 14 * MIB, 18, grid=(4,),
    )


def nothing(*refs):
    pass


def after(value, *before):
    return pl.pallas_call(
        nothing, name="after", out_shape=shaped(value.shape, value.dtype),
        in_specs=[ANY] * (1 + len(before)), out_specs=ANY, input_output_aliases={0: 0},
        compiler_params=pltpu.CompilerParams(vmem_limit_bytes=MIB),
    )(value, *before)


def place(x, y, z, c):
    return ((x % 4 * 4 + y % 4) * 4 + z % 4) * 2 + c


def pairs(step):
    found = []
    for x in range(4):
        for y in range(4):
            for z in range(4):
                for c in range(2):
                    found.append((place(x, y, z, c), step(x, y, z, c)))
    return found


def along_first(r):
    return pairs(lambda x, y, z, c: place(x, y ^ (r * c), z ^ (r * (1 - c)), c))


def along_second(r):
    return pairs(lambda x, y, z, c: place(x, y ^ (r * (1 - c)), z ^ (r * c), c))


def along_x(r):
    return pairs(lambda x, y, z, c: place(x ^ r, y, z, c))


def other_core():
    return pairs(lambda x, y, z, c: place(x, y, z, 1 - c))


def send(values, where):
    return lax.ppermute(values, ALL, where)


def gather_offsets(y, z, c):
    m, j = np.divmod(np.arange(16, dtype=np.int32), 4)

    def of(core):
        row_y = y ^ jnp.where(core == 0, m, j)
        row_z = z ^ jnp.where(core == 0, j, m)
        return ((row_y * 4 + row_z) * 2 + core) * ROWS

    return jnp.concatenate([of(c), of(1 - c)]).astype(jnp.int32)


def scatter_slots(y, z, c):
    block = np.arange(16, dtype=np.int32)
    far_y, far_z = (block // 4) ^ y, (block % 4) ^ z

    def of(core):
        return jnp.where(core == 0, far_z * 4 + far_y, far_y * 4 + far_z)

    return jnp.concatenate([of(c), of(1 - c), c[None]]).astype(jnp.int32)


def zero_of(values):
    return values[(0,) * values.ndim] * 0


def gather_near(shard):
    return jnp.stack([shard] + [send(shard, along_first(r)) for r in (1, 2, 3)])


def gather_far(near):
    halves = near[:2], near[2:]
    first = [send(half, along_second(r)) for half, r in zip(halves, (1, 3))]
    second = [
        send(jnp.stack([half, got]), along_second(r)) for half, got, r in zip(halves, first, (3, 1))
    ]
    return first, second


def gather_pieces(near, first, second, after):
    own = [near, first[0], first[1], second[0].reshape(4, *near.shape[1:]), second[1].reshape(4, *near.shape[1:])]
    return own + [send(piece + after, other_core()) for piece in own]


def gather_direct(near):
    return [near] + [send(near, along_second(r)) for r in (1, 2, 3)]


def with_other(own, after):
    return own + [send(piece + after if i else piece, other_core()) for i, piece in enumerate(own)]


DIRECT = tuple(tuple((r, j) for j in range(4)) for r in range(4))
PIECES = (
    ((0, 0), (0, 1), (0, 2), (0, 3)),
    ((1, 0), (1, 1)),
    ((3, 2), (3, 3)),
    ((3, 0), (3, 1), (2, 0), (2, 1)),
    ((1, 2), (1, 3), (2, 2), (2, 3)),
)
NP = 2 * len(PIECES)
ND = 2 * len(DIRECT)


def total_of(parts):
    summed = parts[0].astype(F32)
    for part in parts[1:]:
        summed = summed + part.astype(F32)
    return summed


def chip_sum(mine, other):
    other = send(other, other_core())
    return [total_of([mine[4 * j : 4 * j + 4], other[4 * j : 4 * j + 4]]).astype(BF16) for j in range(4)]


def scatter_first(groups):
    return [groups[0]] + [send(groups[r], along_first(r)) for r in (1, 2, 3)]


def scatter_rest(near, follow):
    got = [send(near[r], along_second(r)) for r in (1, 2, 3)]
    close = total_of([near[0], after(got[0], follow), *got[1:]]).astype(BF16)
    wide = close.shape[1] // 2
    halves = []
    for half, order in ((close[:, :wide], (1, 3)), (close[:, wide:], (3, 1))):
        half = total_of([half, send(half, along_x(order[0]))]).astype(BF16)
        halves.append(total_of([half, send(half, along_x(order[1]))]))
    return jnp.concatenate(halves, axis=1)


def half_of_chip(values, c):
    return jnp.where(c == 0, values[0], values[1]) + send(jnp.where(c == 0, values[1], values[0]), other_core())


def finish_small(values, rows, c):
    narrow = values.astype(BF16)
    values = total_of([values] + [send(narrow, along_first(r)) for r in (1, 2, 3)])
    other = send(values, other_core())
    mine, late = values[:rows], values[rows:] + other[rows:]
    other = other[:rows]
    return jnp.concatenate([jnp.where(c == 0, mine, other), jnp.where(c == 0, other, mine)]), late


def body(
    tables, log_mel, bucket_list, utterance_frames, stem_weight, first_gain, gate_proj, conv_kernel, second_gain,
    out_proj, cotangent,
):
    y, z, c = lax.axis_index("y"), lax.axis_index("z"), lax.axis_index("c")
    offsets = gather_offsets(y, z, c)
    slots = scatter_slots(y, z, c)
    tables = {name: jnp.asarray(value) for name, value in tables.items()}
    first_gain, second_gain = first_gain[None], second_gain[None]

    gate_near = gather_near(gate_proj)
    outgoing = jnp.take(log_mel, bucket_list[0], axis=0) + zero_of(gate_near[1])
    arrived = lax.all_to_all(outgoing, ALL, split_axis=0, concat_axis=0, tiled=True)
    gate_far = gather_far(gate_near)
    stem_total, embedded, normed, normed_t, frames_t, spectrum, mix_grad = stem(
        gate_far[0][0], arrived.reshape(TOK * PATCH, MEL), utterance_frames, stem_weight, first_gain, conv_kernel, cotangent, tables
    )
    gate_pieces = gather_pieces(gate_near, *gate_far, zero_of(normed))
    out_near = gather_near(out_proj + zero_of(gate_far[0][0])) + sum(zero_of(piece) for piece in gate_far[1])
    out_own = gather_direct(out_near)
    value, gate, filtered = gate_forward(offsets, utterance_frames, gate_pieces, normed, spectrum, tables)
    out_pieces = with_other(out_own, zero_of(filtered).astype(BF16))
    out_mine, out_other, swished = out_grad(slots, out_own[1:], filtered, mix_grad, second_gain)
    filter_grad, second_grad = middle(offsets, out_pieces, filtered, mix_grad, second_gain)
    out_sums = chip_sum(out_mine, out_other)
    out_groups = scatter_first(out_sums)
    grads, nears, convs = [], [], []
    for begin, count in ((0, 4), (4, 2)):
        value_grad, gate_grad, mine, other, conv_grad = conv_back(
            slots, utterance_frames, out_sums[1:], value, gate, filter_grad, normed_t, spectrum, tables, begin, count
        )
        grads.append((value_grad, gate_grad))
        if begin:
            other = after(other, *out_groups[1:])
        nears.append((mine, send(other, other_core())))
        convs.append(conv_grad[:TAPS])
    gate_groups = chip_sums(nears)
    first_grad, stem_grad = stem_back(
        offsets, utterance_frames, gate_pieces, [pair[k] for k in range(2) for pair in grads], gate_groups[1:], embedded,
        stem_total, mix_grad, first_gain, frames_t,
    )
    early = jnp.concatenate([jnp.concatenate(convs, axis=1), second_grad], axis=0)
    early = half_of_chip(early.reshape(2, 16, D), c)
    follow = zero_of(first_grad)
    terms = [scatter_first(gate_groups), out_groups]
    near = jnp.concatenate([(total_of(term) + follow).astype(BF16) for term in terms], axis=-1)
    late = jnp.concatenate([first_grad, jnp.pad(stem_grad.reshape(1, -1), ((0, 0), (0, D - 16 * CH)))], axis=0)
    small = jnp.concatenate([early, late, jnp.zeros((6, D), F32)], axis=0)
    small = jnp.concatenate([small[:8], small[8:16], small[16:]], axis=1).astype(BF16)
    near = jnp.concatenate([near, jnp.broadcast_to(small[None], (4, *small.shape))], axis=1)
    output = mixed_out(offsets, utterance_frames, out_pieces, near, swished, embedded)
    sums = scatter_rest(near, output)
    small = sums[ROWS:]
    early, late = finish_small(
        jnp.concatenate([small[:, :D], small[:, D : 2 * D], small[:2, 2 * D :]]), 16, c
    )
    sums = sums[:ROWS]
    blocks = [sums[:, i * CB : (i + 1) * CB] for i in range(2 * NB)]
    gate_sums = jnp.concatenate(blocks[::2] + blocks[1::2], axis=1)
    return (
        output, gate_sums, sums[:, 2 * D :], late[1, : 16 * CH].reshape(16, CH), late[0],
        early[:TAPS], early[TAPS],
    )


def solution(mesh):
    grid = Mesh(mesh.devices.reshape(4, 4, 4, 2), ALL)
    rows = ("y", "z", "c")
    return jax.shard_map(
        functools.partial(body, transforms()),
        mesh=grid,
        in_specs=(
            P(ALL, None, None), P(ALL, None), P(ALL), P(), P(), P(rows, None), P(), P(), P(rows, None), P(ALL, None),
        ),
        out_specs=(P(ALL, None), P(rows, None), P(rows, None), P(), P(), P(), P()),
        check_vma=False,
    )
```
